512 devices in a mesh: row: 16 (over x, z_lo), col: 32 (over y, z_hi, core).
Axes of the slice: x: 4, y: 8, z: 8 (z_hi: 2, z_lo: 4; z = z_hi * 4 + z_lo), core: 2. Of those that a mesh axis runs over, the one named last changes fastest.
Arguments:
- pair: bfloat16 [384, 384, 128], P('row', 'col'), may hold values from -6 to 6
- cotangent: bfloat16 [384, 384, 128], P('row', 'col'), may hold values from -6 to 6
- chain_counts: int32 [4], replicated, may hold values from 48 to 96
- in_gain: float32 [128], replicated, may hold values from 0.1 to 1.9
- in_bias: float32 [128], replicated, may hold values from -0.5 to 0.5
- w_values: bfloat16 [128, 256], replicated, may hold values from -0.5 to 0.5
- w_gates: bfloat16 [128, 256], replicated, may hold values from -0.5 to 0.5
- w_out_gate: bfloat16 [128, 128], replicated, may hold values from -0.5 to 0.5
- out_gain: float32 [128], replicated, may hold values from 0.1 to 1.9
- out_bias: float32 [128], replicated, may hold values from -0.5 to 0.5
- w_out: bfloat16 [128, 128], replicated, may hold values from -0.5 to 0.5
Outputs:
- update: bfloat16 [384, 384, 128], P('row', 'col')
- grad_pair: bfloat16 [384, 384, 128], P('row', 'col')
The draws below stay inside these ranges and needn't reach their ends.
Inputs may be any that keep to these rules, and one draw needn't show every extreme that they name: Tokens at positions from the sum of chain_counts onward are padding.
All inputs are finite; a program needn't handle non-finite values.
Results may differ from the reference program's by a relative error of at most 0.0078.
Values may be sent and summed in bfloat16 or wider, within the bound.
No kernel may reach another device: no remote copies, remote signals or barrier semaphores. Data moves between devices by JAX's collectives and lax.ppermute only.
A program may use at most 64 MiB of HBM per device.

```python
import jax
import jax.numpy as jnp
from jax import lax

C = 128
H = 128
CHAINS = 4
TOKENS = 384


def plant(array, rng, least, largest):
    place = [jax.random.randint(jax.random.fold_in(rng, axis), (), 0, length) for axis, length in enumerate(array.shape)]
    longest = array.shape.index(max(array.shape))
    beside = place[:longest] + [(place[longest] + 1) % array.shape[longest]] + place[longest + 1:]
    return array.at[tuple(place)].set(least).at[tuple(beside)].set(largest)


def shard_levels(own_key, extent, cuts, least, high):
    def one(position, parts):
        steps = jax.random.uniform(jax.random.fold_in(jax.random.fold_in(own_key, 6), position), (parts,), jnp.float32, least / len(cuts), high / len(cuts))
        return jnp.repeat(jnp.exp(steps), extent[position] // parts).reshape((-1,) + (1,) * (len(extent) - position - 1))

    factor_of = one(*cuts[0])
    for cut in cuts[1:]:
        factor_of = factor_of * one(*cut)
    return factor_of


def gaussian(rng, extent, scale, reach, shards=(), held_as=jnp.bfloat16):
    values = scale * jax.random.normal(rng, extent, jnp.float32)
    if shards:
        values = values * shard_levels(rng, extent, shards, -0.22, 0.18)
    return jnp.clip(values, -reach, reach).astype(held_as)


def setup_inputs(seed: int = 0) -> dict:
    keys = jax.random.split(jax.random.key(seed), 12)
    pair = gaussian(keys[0], (TOKENS, TOKENS, C), 1.0, 6.0, ((0, 16), (1, 32)))
    cotangent = gaussian(keys[1], (TOKENS, TOKENS, C), 1.0, 6.0, ((0, 16), (1, 32)))
    chain_counts = plant(jax.random.randint(keys[2], (CHAINS,), TOKENS // (2 * CHAINS), TOKENS // CHAINS + 1), jax.random.fold_in(keys[2], 1), TOKENS // (2 * CHAINS), (TOKENS // CHAINS + 1) - 1).astype(jnp.int32)
    in_gain = jnp.clip(1.0 + 0.18 * jax.random.normal(keys[3], (C,), jnp.float32), 0.1, 1.9)
    in_bias = jnp.clip(jax.random.uniform(keys[4], (C,), jnp.float32, -0.5, 0.5), -0.5, 0.5)
    w_values = gaussian(keys[5], (C, 2 * H), C ** -0.5, 0.5)
    w_gates = gaussian(keys[6], (C, 2 * H), C ** -0.5, 0.5)
    w_out_gate = gaussian(keys[7], (C, C), C ** -0.5, 0.5)
    out_gain = jnp.clip(1.0 + 0.18 * jax.random.normal(keys[8], (H,), jnp.float32), 0.1, 1.9)
    out_bias = jnp.clip(jax.random.uniform(keys[9], (H,), jnp.float32, -0.5, 0.5), -0.5, 0.5)
    w_out = gaussian(keys[10], (H, C), H ** -0.5, 0.5)
    return {"pair": pair, "cotangent": cotangent, "chain_counts": chain_counts, "in_gain": in_gain, "in_bias": in_bias, "w_values": w_values, "w_gates": w_gates, "w_out_gate": w_out_gate, "out_gain": out_gain, "out_bias": out_bias, "w_out": w_out}


EPS = 1e-05

def layer_norm(values_in, scale_vec, shift_vec):
    centre = values_in - lax.optimization_barrier(jnp.mean(values_in, axis=-1, keepdims=True))
    inv_std = lax.rsqrt(lax.optimization_barrier(jnp.mean(centre * centre, axis=-1, keepdims=True)) + EPS)
    normed_hat = centre * inv_std
    return (normed_hat * scale_vec + shift_vec, normed_hat, inv_std)

def norm_back(upstream, scale_vec, normed_hat, inv_std):
    scaled = upstream * scale_vec
    first_mean = lax.optimization_barrier(jnp.mean(scaled, axis=-1, keepdims=True))
    second_mean = lax.optimization_barrier(jnp.mean(scaled * normed_hat, axis=-1, keepdims=True))
    return inv_std * (scaled - first_mean - normed_hat * second_mean)

def reference(pair, cotangent, chain_counts, in_gain, in_bias, w_values, w_gates, w_out_gate, out_gain, out_bias, w_out):
    pair_full = pair.astype(jnp.float32)
    normed, pair_hat, pair_inv = layer_norm(pair_full, in_gain, in_bias)
    normed_b = normed.astype(jnp.bfloat16)
    valid_count = jnp.sum(chain_counts).astype(jnp.int32)
    positions = jnp.arange(TOKENS, dtype=jnp.int32)
    live = (positions < valid_count).astype(jnp.float32)
    pair_mask = (live[:, None] * live[None, :])[..., None]
    values = jnp.dot(normed_b, w_values, preferred_element_type=jnp.float32)
    gate_sig = jax.nn.sigmoid(jnp.dot(normed_b, w_gates, preferred_element_type=jnp.float32))
    both = (gate_sig * values * pair_mask).astype(jnp.bfloat16)
    both = lax.optimization_barrier(both)
    left = both[..., :H].astype(jnp.float32)
    right = both[..., H:].astype(jnp.float32)
    inner = jnp.einsum('ikh,jkh->ijh', left, right)
    inner_n, inner_hat, inner_inv = layer_norm(inner, out_gain, out_bias)
    inner_b = inner_n.astype(jnp.bfloat16)
    proj_out = jnp.dot(inner_b, w_out, preferred_element_type=jnp.float32)
    out_sig = jax.nn.sigmoid(jnp.dot(normed_b, w_out_gate, preferred_element_type=jnp.float32))
    update = (out_sig * proj_out).astype(jnp.bfloat16)
    upstream = cotangent.astype(jnp.float32)
    d_proj = (upstream * out_sig).astype(jnp.bfloat16)
    d_gate_out = (upstream * proj_out * out_sig * (1.0 - out_sig)).astype(jnp.bfloat16)
    d_inner_n = jnp.dot(d_proj, w_out.T, preferred_element_type=jnp.float32)
    d_inner = norm_back(d_inner_n, out_gain, inner_hat, inner_inv).astype(jnp.bfloat16)
    d_inner = lax.optimization_barrier(d_inner)
    d_inner_f = d_inner.astype(jnp.float32)
    d_left = jnp.einsum('ijh,jkh->ikh', d_inner_f, right)
    d_right = jnp.einsum('ijh,ikh->jkh', d_inner_f, left)
    d_both = jnp.concatenate([d_left, d_right], axis=-1) * pair_mask
    d_values = (d_both * gate_sig).astype(jnp.bfloat16)
    d_gates = (d_both * values * gate_sig * (1.0 - gate_sig)).astype(jnp.bfloat16)
    d_normed = jnp.dot(d_values, w_values.T, preferred_element_type=jnp.float32)
    d_normed = d_normed + jnp.dot(d_gates, w_gates.T, preferred_element_type=jnp.float32)
    d_normed = d_normed + jnp.dot(d_gate_out, w_out_gate.T, preferred_element_type=jnp.float32)
    grad_pair = norm_back(d_normed, in_gain, pair_hat, pair_inv).astype(jnp.bfloat16)
    return (update, grad_pair)
```

```python
import jax
import jax.numpy as jnp
from jax import lax
from jax.sharding import Mesh
from jax.sharding import PartitionSpec as P

EPS = 1e-05
ROW = ("x", "z_lo")
COL = ("y", "z_hi", "core")
GROUP = ("x", "z_lo", "y")
ALL = ROW + COL


def layer_norm(values_in, scale_vec, shift_vec, axis):
    centre = values_in - jnp.mean(values_in, axis=axis, keepdims=True)
    inv_std = lax.rsqrt(jnp.mean(centre * centre, axis=axis, keepdims=True) + EPS)
    normed_hat = centre * inv_std
    return (normed_hat * scale_vec + shift_vec, normed_hat, inv_std)


def norm_back(upstream, scale_vec, normed_hat, inv_std, axis):
    scaled = upstream * scale_vec
    first_mean = jnp.mean(scaled, axis=axis, keepdims=True)
    second_mean = jnp.mean(scaled * normed_hat, axis=axis, keepdims=True)
    return inv_std * (scaled - first_mean - normed_hat * second_mean)


def dot(a, b, contract):
    return lax.dot_general(a, b, ((contract[:1], contract[1:]), ((), ())), preferred_element_type=jnp.float32)


def shards(
    pair,
    cotangent,
    chain_counts,
    in_gain,
    in_bias,
    w_values,
    w_gates,
    w_out_gate,
    out_gain,
    out_bias,
    w_out,
):
    rows_here, cols_here, width = pair.shape
    hidden = w_out.shape[0]
    here = rows_here * cols_here
    n_rows = lax.axis_size(ROW)
    n_cols = lax.axis_size(COL)
    n_parts = n_cols // lax.axis_size("y")
    n_y = lax.axis_size("y")
    tokens = n_rows * rows_here
    valid_count = jnp.sum(chain_counts)
    row_ids = lax.axis_index(ROW) * rows_here + jnp.arange(rows_here, dtype=jnp.int32)
    col_ids = lax.axis_index(COL) * cols_here + jnp.arange(cols_here, dtype=jnp.int32)
    row_live = (row_ids < valid_count).astype(jnp.float32)
    col_live = (col_ids < valid_count).astype(jnp.float32)
    pair_mask = (row_live[:, None] * col_live[None, :]).reshape(1, here)

    pair_full = pair.reshape(here, width).astype(jnp.float32)
    normed, pair_hat, pair_inv = layer_norm(pair_full, in_gain, in_bias, 1)
    normed_b = normed.astype(jnp.bfloat16)
    w_front = jnp.concatenate([w_values, w_gates, w_out_gate], axis=1)
    front = dot(w_front, normed_b, (0, 1))
    values = front[: 2 * hidden]
    gate_sig = jax.nn.sigmoid(front[2 * hidden : 4 * hidden])
    out_sig = jax.nn.sigmoid(front[4 * hidden :])
    both = (gate_sig * values * pair_mask).astype(jnp.bfloat16)
    both = jnp.stack([both[:hidden], both[hidden:]], axis=1)
    both = lax.all_to_all(both, GROUP, 0, 0)

    def to_matrix(blocks):
        blocks = blocks.reshape(n_rows, -1, rows_here, cols_here)
        return blocks.transpose(0, 2, 1, 3).reshape(tokens, -1)

    def to_blocks(matrix):
        matrix = matrix.reshape(n_rows, rows_here, -1, cols_here)
        return matrix.transpose(0, 2, 1, 3).reshape(-1, here)

    left, right = to_matrix(both[:, 0]), to_matrix(both[:, 1])
    inner = to_blocks(dot(left, right, (1, 1)).astype(jnp.bfloat16))
    inner = lax.all_to_all(inner, ALL, 0, 0).reshape(hidden, n_parts, here)
    inner = jnp.sum(inner.astype(jnp.float32), axis=1)

    inner_n, inner_hat, inner_inv = layer_norm(inner, out_gain[:, None], out_bias[:, None], 0)
    inner_b = inner_n.astype(jnp.bfloat16)
    proj_out = dot(w_out, inner_b, (0, 0))
    update = (out_sig * proj_out).T.astype(jnp.bfloat16)
    upstream = cotangent.reshape(here, width).T.astype(jnp.float32)
    d_proj = (upstream * out_sig).astype(jnp.bfloat16)
    d_gate_out = (upstream * proj_out * out_sig * (1.0 - out_sig)).astype(jnp.bfloat16)
    d_inner_n = dot(w_out, d_proj, (1, 0))
    d_inner = norm_back(d_inner_n, out_gain[:, None], inner_hat, inner_inv, 0).astype(jnp.bfloat16)

    d_inner = jnp.broadcast_to(d_inner[:, None], (hidden, n_parts, here)).reshape(-1, here)
    d_inner = to_matrix(lax.all_to_all(d_inner, ALL, 0, 0))
    d_left = dot(d_inner, right, (1, 0)).astype(jnp.bfloat16)
    d_right = dot(d_inner, left, (0, 0)).astype(jnp.bfloat16)
    d_both = jnp.stack([to_blocks(d_left), to_blocks(d_right)], axis=1)
    d_both = lax.all_to_all(d_both, GROUP, 0, 0).astype(jnp.float32)

    d_both = jnp.concatenate([d_both[:, 0], d_both[:, 1]], axis=0) * pair_mask
    d_values = (d_both * gate_sig).astype(jnp.bfloat16)
    d_gates = (d_both * values * gate_sig * (1.0 - gate_sig)).astype(jnp.bfloat16)
    d_front = jnp.concatenate([d_values, d_gates, d_gate_out], axis=0)
    d_normed = dot(d_front, w_front, (0, 1))
    grad_pair = norm_back(d_normed, in_gain, pair_hat, pair_inv, 1).astype(jnp.bfloat16)
    return (update.reshape(pair.shape), grad_pair.reshape(pair.shape))


def solution(mesh):
    fine = Mesh(mesh.devices.reshape(4, 4, 8, 2, 2), ALL)
    placed = P(ROW, COL, None)
    return jax.shard_map(
        shards,
        mesh=fine,
        in_specs=(placed, placed) + (P(),) * 9,
        out_specs=(placed, placed),
        check_vma=False,
    )
```

```python
import jax
import jax.numpy as jnp
from jax import lax
from jax.experimental import pallas as pl
from jax.experimental.pallas import tpu as pltpu
from jax.sharding import Mesh
from jax.sharding import PartitionSpec as P

EPS = 1e-05
F32 = jnp.float32
BF16 = jnp.bfloat16
ROW = ("x", "z_lo")
COL = ("y", "z_hi", "core")
GROUP = ("z_lo",) + COL
SLOT = 16
SWAP = 8


def dot(a, b, contract):
    return lax.dot_general(a, b, ((contract[:1], contract[1:]), ((), ())), preferred_element_type=F32)


def swap_groups(x):
    sub = lax.broadcasted_iota(jnp.int32, x.shape, 1)
    group = lax.broadcasted_iota(jnp.int32, x.shape, 2) // SLOT
    for step in (4, 2, 1):
        up = pltpu.roll(pltpu.roll(x, SWAP - step, 1), SLOT * step, 2)
        down = up if step == 4 else pltpu.roll(pltpu.roll(x, step, 1), 128 - SLOT * step, 2)
        sub_bit, group_bit = (sub & step) != 0, (group & step) != 0
        x = jnp.where(sub_bit == group_bit, x, jnp.where(group_bit, up, down))
    return x


def to_matrix(blocks, out):
    for i_hi in range(3):
        part = blocks[:, 128 * i_hi : 128 * (i_hi + 1)].reshape(16, 8, 128)
        part = swap_groups(part)
        for z in range(4):
            for c_hi in range(4):
                row = 24 * z + 8 * i_hi
                out[row : row + 8, 128 * c_hi : 128 * (c_hi + 1)] = part[4 * z + c_hi]


def to_blocks(matrix, out):
    for i_hi in range(3):
        for z in range(4):
            row = 24 * z + 8 * i_hi
            part = jnp.stack([matrix[row : row + 8, 128 * c : 128 * (c + 1)] for c in range(4)])
            part = swap_groups(part).reshape(32, 128)
            out[32 * z : 32 * (z + 1), 128 * i_hi : 128 * (i_hi + 1)] = part


def spread():
    token = lax.broadcasted_iota(jnp.int32, (384, 512), 0)
    lane = lax.broadcasted_iota(jnp.int32, (384, 512), 1)
    slot = lane % SLOT
    hit = (token == lane // SLOT * 12 + slot) & (slot < 12)
    return hit.astype(F32).astype(BF16)


def live_mask(counts):
    valid = counts[0] + counts[1] + counts[2] + counts[3]
    lane = lax.broadcasted_iota(jnp.int32, (1, 384), 1)
    i, j = lane // SLOT, lane % SLOT
    row = lax.axis_index("x") * 4 + lax.axis_index("z_lo")
    col = lax.axis_index("y") * 4 + lax.axis_index("z_hi") * 2 + lax.axis_index("core")
    live = (row * 24 + i < valid) & (col * 12 + j < valid) & (j < 12)
    return live.astype(F32)


def column(vector, width):
    square = jnp.broadcast_to(vector.reshape(1, 128), (128, 128)).T
    return jnp.concatenate([square] * (width // 128), axis=1)


def load_tile(tile, scratch):
    scratch[...] = jnp.zeros_like(scratch)
    scratch[:, :12, :] = tile[...].astype(F32)
    return scratch[...].reshape(384, 128)


def front_kernel(counts, pair, gain, bias, w_values, w_gates, both, values, gate, hat, inv, normed, tile):
    x = load_tile(pair, tile)
    centre = x - jnp.mean(x, axis=1, keepdims=True)
    inv_std = lax.rsqrt(jnp.mean(centre * centre, axis=1, keepdims=True) + EPS)
    pair_hat = centre * inv_std
    normed_b = (pair_hat * gain[...].reshape(1, 128) + bias[...].reshape(1, 128)).astype(BF16)
    hat[...] = pair_hat
    inv[...] = jnp.broadcast_to(inv_std, (384, 128))
    normed[...] = normed_b
    vals = dot(w_values[...], normed_b, (0, 1))
    sig = jax.nn.sigmoid(dot(w_gates[...], normed_b, (0, 1)))
    values[...] = vals
    gate[...] = sig
    out = (sig * vals * live_mask(counts)).astype(BF16)
    both[:, :384] = out[:128]
    both[:, 384:] = out[128:]


def gate_kernel(normed, cotangent, w_out_gate, w_out, out_gain, out_sig, upstream, scaled, tile):
    sig = jax.nn.sigmoid(dot(w_out_gate[...], normed[...], (0, 1)))
    up = load_tile(cotangent, tile).T
    d_proj = (up * sig).astype(BF16)
    out_sig[...] = sig
    upstream[...] = up
    scaled[...] = dot(w_out[...], d_proj, (1, 0)) * column(out_gain[...], 384)


def split_kernel(both, left, right, matrix):
    to_matrix(both[:, :384].astype(F32), matrix)
    left[...] = matrix[...].astype(BF16)
    to_matrix(both[:, 384:].astype(F32), matrix)
    rounded = matrix[...].astype(BF16)
    for part in range(4):
        right[part] = rounded


def inner_kernel(left, right, inner, blocks):
    product = dot(left[...], right[...].reshape(384, 512), (1, 1)).astype(BF16)
    to_blocks(dot(product, spread(), (1, 0)), blocks)
    inner[...] = blocks[...].astype(BF16)


def norm_kernel(inner, scaled, out_gain, out_bias, d_inner, inner_b):
    x = inner[...].astype(F32)
    centre = x - jnp.mean(x, axis=0, keepdims=True)
    inv_std = lax.rsqrt(jnp.mean(centre * centre, axis=0, keepdims=True) + EPS)
    hat = centre * inv_std
    up = scaled[...]
    first_mean = jnp.mean(up, axis=0, keepdims=True)
    second_mean = jnp.mean(up * hat, axis=0, keepdims=True)
    d_inner[...] = (inv_std * (up - first_mean - hat * second_mean)).astype(BF16)
    inner_b[...] = (hat * column(out_gain[...], 384) + column(out_bias[...], 384)).astype(BF16)


def update_kernel(inner_b, out_sig, upstream, w_out, w_out_gate, update, d_normed):
    proj = dot(w_out[...], inner_b[...], (0, 0))
    sig = out_sig[...]
    gated = (sig * proj).T.reshape(24, SLOT, 128)
    update[...] = gated[:, :12, :].astype(BF16)
    d_gate_out = (upstream[...] * proj * sig * (1.0 - sig)).astype(BF16)
    d_normed[...] = dot(d_gate_out, w_out_gate[...], (0, 1))


def grad_kernel(d_inner, left, right, d_left, d_right, matrix):
    to_matrix(d_inner[...].astype(F32), matrix)
    packed = dot(matrix[...].astype(BF16), spread(), (1, 1)).astype(BF16)
    d_left[...] = dot(packed, right[...].reshape(384, 512), (1, 0))
    d_right[...] = dot(packed, left[...], (0, 0)).astype(BF16).reshape(4, 96, 512)


def merge_kernel(d_left, d_right, d_both, blocks):
    to_blocks(d_left[...], blocks)
    d_both[:, :384] = blocks[...].astype(BF16)
    parts = [d_right[part].astype(F32) for part in range(4)]
    to_blocks((parts[0] + parts[1]) + (parts[2] + parts[3]), blocks)
    d_both[:, 384:] = blocks[...].astype(BF16)


def back_kernel(counts, d_both, values, gate, d_out, hat, inv, gain, w_values, w_gates, grad):
    live = live_mask(counts)
    incoming = jnp.concatenate([d_both[:, :384], d_both[:, 384:]], axis=0).astype(F32) * live
    sig = gate[...]
    d_values = (incoming * sig).astype(BF16)
    d_gates = (incoming * values[...] * sig * (1.0 - sig)).astype(BF16)
    d_normed = d_out[...] + dot(d_values, w_values[...], (0, 1)) + dot(d_gates, w_gates[...], (0, 1))
    scaled = d_normed * gain[...].reshape(1, 128)
    pair_hat = hat[...]
    first_mean = jnp.mean(scaled, axis=1, keepdims=True)
    second_mean = jnp.mean(scaled * pair_hat, axis=1, keepdims=True)
    out = inv[...] * (scaled - first_mean - pair_hat * second_mean)
    grad[...] = out.reshape(24, SLOT, 128)[:, :12, :].astype(BF16)


def call(kernel, outs, args, scratch=(), scalars=0, flops=0):
    vmem, smem = pl.BlockSpec(memory_space=pltpu.VMEM), pl.BlockSpec(memory_space=pltpu.SMEM)
    outs = [jax.ShapeDtypeStruct(shape, dtype) for shape, dtype in outs]
    size = sum(a.size * a.dtype.itemsize for a in list(args) + outs)
    return pl.pallas_call(
        kernel,
        out_shape=outs,
        in_specs=[smem] * scalars + [vmem] * (len(args) - scalars),
        out_specs=[vmem] * len(outs),
        scratch_shapes=[pltpu.VMEM(shape, F32) for shape in scratch],
        compiler_params=pltpu.CompilerParams(vmem_limit_bytes=24 * 1024 * 1024),
        cost_estimate=pl.CostEstimate(flops=flops, bytes_accessed=size, transcendentals=0),
    )(*args)


def shards(
    pair,
    cotangent,
    chain_counts,
    in_gain,
    in_bias,
    w_values,
    w_gates,
    w_out_gate,
    out_gain,
    out_bias,
    w_out,
):
    wide, tall = (256, 384), (128, 384)
    tile = (24, SLOT, 128)
    both, values, gate, hat, inv, normed = call(
        front_kernel,
        [((128, 768), BF16), (wide, F32), (wide, F32), ((384, 128), F32), ((384, 128), F32), ((384, 128), BF16)],
        [chain_counts, pair, in_gain, in_bias, w_values, w_gates],
        [tile],
        scalars=1,
    )
    both = lax.all_to_all(both, GROUP, 0, 0)
    out_sig, upstream, scaled = call(
        gate_kernel,
        [(tall, F32)] * 3,
        [normed, cotangent, w_out_gate, w_out, out_gain],
        [tile],
    )
    left, right = call(split_kernel, [((96, 512), BF16), ((4, 96, 512), BF16)], [both], [(96, 512)])
    right = lax.all_to_all(right, "x", 0, 0)
    (inner,) = call(inner_kernel, [(tall, BF16)], [left, right], [tall])
    inner = lax.all_to_all(inner, GROUP, 0, 0)
    d_inner, inner_b = call(norm_kernel, [(tall, BF16)] * 2, [inner, scaled, out_gain, out_bias])
    d_inner = lax.all_to_all(d_inner, GROUP, 0, 0)
    update, d_out = call(
        update_kernel,
        [(pair.shape, BF16), ((384, 128), F32)],
        [inner_b, out_sig, upstream, w_out, w_out_gate],
    )
    d_left, d_right = call(
        grad_kernel, [((96, 512), F32), ((4, 96, 512), BF16)], [d_inner, left, right], [(96, 512)]
    )
    d_right = lax.all_to_all(d_right, "x", 0, 0)
    (d_both,) = call(merge_kernel, [((128, 768), BF16)], [d_left, d_right], [tall])
    d_both = lax.all_to_all(d_both, GROUP, 0, 0)
    (grad,) = call(
        back_kernel,
        [(pair.shape, BF16)],
        [chain_counts, d_both, values, gate, d_out, hat, inv, in_gain, w_values, w_gates],
        scalars=1,
    )
    return (update, grad)


def solution(mesh):
    fine = Mesh(mesh.devices.reshape(4, 4, 8, 2, 2), ROW + COL)
    placed = P(ROW, COL, None)
    return jax.shard_map(
        shards,
        mesh=fine,
        in_specs=(placed, placed) + (P(),) * 9,
        out_specs=(placed, placed),
        check_vma=False,
    )
```

```python
import jax
import jax.numpy as jnp
from jax import lax
from jax.experimental import pallas as pl
from jax.experimental.pallas import tpu as pltpu
from jax.sharding import Mesh
from jax.sharding import PartitionSpec as P

EPS = 1e-05
F32 = jnp.float32
BF16 = jnp.bfloat16
ROW = ("x", "z_lo")
COL = ("y", "z_hi", "core")
GROUP = ("z_lo",) + COL
SLOTS = 16
LOW = 8


def dot(a, b, contract):
    return lax.dot_general(a, b, ((contract[:1], contract[1:]), ((), ())), preferred_element_type=F32)


def swap_groups(x):
    sub = lax.broadcasted_iota(jnp.int32, x.shape, 1)
    lane = lax.broadcasted_iota(jnp.int32, x.shape, 2)
    for step in (4, 2, 1):
        up = pltpu.roll(pltpu.roll(x, LOW - step, 1), step, 2)
        down = pltpu.roll(pltpu.roll(x, step, 1), 128 - step, 2)
        sub_bit, lane_bit = (sub & step) != 0, (lane & step) != 0
        x = jnp.where(sub_bit == lane_bit, x, jnp.where(lane_bit, up, down))
    return x


def to_matrix(rows, first, per, out):
    for i_hi in range(3):
        part = rows[pl.ds(first + i_hi, 128, stride=per), :].reshape(16, LOW, 128)
        part = swap_groups(part)
        for z in range(4):
            for c_hi in range(4):
                row = 24 * z + LOW * i_hi
                out[row : row + LOW, 128 * c_hi : 128 * (c_hi + 1)] = part[4 * z + c_hi]


def to_rows(matrix, rows, first, per):
    for i_hi in range(3):
        parts = []
        for z in range(4):
            row = 24 * z + LOW * i_hi
            parts += [matrix[row : row + LOW, 128 * c : 128 * (c + 1)] for c in range(4)]
        rows[pl.ds(first + i_hi, 128, stride=per), :] = swap_groups(jnp.stack(parts)).reshape(128, 128)


def spread():
    lane = lax.broadcasted_iota(jnp.int32, (1, 512), 1)
    slot = lane % 128 // LOW
    token = (lane // 128 * LOW + lane % LOW) * 12 + slot
    token = jnp.where(slot < 12, token, -1)
    hit = lax.broadcasted_iota(jnp.int32, (384, 512), 0) == token
    return jnp.where(hit, 1.0, 0.0).astype(BF16)


def live_mask(counts):
    valid = counts[0] + counts[1] + counts[2] + counts[3]
    lane = lax.broadcasted_iota(jnp.int32, (1, 384), 1)
    i, j = lane // 128 * LOW + lane % LOW, lane % 128 // LOW
    row = lax.axis_index("x") * 4 + lax.axis_index("z_lo")
    col = lax.axis_index("y") * 4 + lax.axis_index("z_hi") * 2 + lax.axis_index("core")
    live = (row * 24 + i < valid) & (col * 12 + j < valid) & (j < 12)
    return live.astype(F32)


def column(vector, width):
    square = jnp.broadcast_to(vector.reshape(1, 128), (128, 128)).T
    return jnp.concatenate([square] * (width // 128), axis=1)


def load_tile(tile):
    x = tile[...].astype(F32)
    gap = jnp.zeros(((SLOTS - 12) * LOW, 128), F32)
    parts = []
    for i_hi in range(3):
        parts += [x[:, LOW * i_hi : LOW * (i_hi + 1)].reshape(12 * LOW, 128), gap]
    return jnp.concatenate(parts, axis=0)


def store_tile(value, scratch, tile):
    for i_hi in range(3):
        part = value[128 * i_hi : 128 * i_hi + 12 * LOW].reshape(12, LOW, 128)
        scratch[:, LOW * i_hi : LOW * (i_hi + 1), :] = part
    tile[...] = scratch[...].astype(BF16)


def third(value, i_hi):
    return value[:, 128 * i_hi : 128 * (i_hi + 1)]


def front_kernel(counts, pair, gain, bias, w_values, w_gates, both, values, gate, hat, inv, normed, rows):
    x = load_tile(pair)
    centre = x - jnp.mean(x, axis=1, keepdims=True)
    inv_std = lax.rsqrt(jnp.mean(centre * centre, axis=1, keepdims=True) + EPS)
    pair_hat = centre * inv_std
    normed_b = (pair_hat * gain[...].reshape(1, 128) + bias[...].reshape(1, 128)).astype(BF16)
    hat[...] = pair_hat
    inv[...] = jnp.broadcast_to(inv_std, (384, 128))
    normed[...] = normed_b
    vals = dot(w_values[...], normed_b, (0, 1))
    sig = jax.nn.sigmoid(dot(w_gates[...], normed_b, (0, 1)))
    values[...] = vals
    gate[...] = sig
    out = sig * vals * live_mask(counts)
    for i_hi in range(3):
        rows[pl.ds(i_hi, 128, stride=8), :] = third(out[:128], i_hi)
        rows[pl.ds(3 + i_hi, 128, stride=8), :] = third(out[128:], i_hi)
    for spare in (6, 7):
        rows[pl.ds(spare, 128, stride=8), :] = jnp.zeros((128, 128), F32)
    both[...] = rows[...].astype(BF16)


def gate_kernel(normed, cotangent, w_out_gate, w_out, out_gain, out_sig, upstream, scaled):
    sig = jax.nn.sigmoid(dot(w_out_gate[...], normed[...], (0, 1)))
    up = load_tile(cotangent).T
    d_proj = (up * sig).astype(BF16)
    out_sig[...] = sig
    upstream[...] = up
    scaled[...] = dot(w_out[...], d_proj, (1, 0)) * column(out_gain[...], 384)


def split_kernel(both, left, right, rows, matrix):
    rows[...] = both[...].astype(F32)
    one_hot = spread()
    to_matrix(rows, 0, 8, matrix)
    left[...] = dot(matrix[...].astype(BF16), one_hot, (1, 1)).astype(BF16)
    to_matrix(rows, 3, 8, matrix)
    packed = dot(matrix[...].astype(BF16), one_hot, (1, 1)).astype(BF16)
    for part in range(4):
        right[part] = packed


def inner_kernel(left, right, inner, rows):
    product = dot(left[...], right[...].reshape(384, 384), (1, 1)).astype(BF16)
    to_rows(dot(product, spread(), (1, 0)), rows, 0, 4)
    rows[pl.ds(3, 128, stride=4), :] = jnp.zeros((128, 128), F32)
    inner[...] = rows[...].astype(BF16)


def norm_kernel(inner, scaled, d_inner, inner_hat, rows):
    rows[...] = inner[...].astype(F32)
    for i_hi in range(3):
        x = rows[pl.ds(i_hi, 128, stride=4), :]
        centre = x - jnp.mean(x, axis=0, keepdims=True)
        inv_std = lax.rsqrt(jnp.mean(centre * centre, axis=0, keepdims=True) + EPS)
        hat = centre * inv_std
        up = scaled[:, 128 * i_hi : 128 * (i_hi + 1)]
        first_mean = jnp.mean(up, axis=0, keepdims=True)
        second_mean = jnp.mean(up * hat, axis=0, keepdims=True)
        rows[pl.ds(i_hi, 128, stride=4), :] = inv_std * (up - first_mean - hat * second_mean)
        inner_hat[:, 128 * i_hi : 128 * (i_hi + 1)] = hat
    d_inner[...] = rows[...].astype(BF16)


def update_kernel(inner_hat, out_sig, upstream, out_gain, out_bias, w_out, w_out_gate, update, d_normed, tile):
    inner_n = inner_hat[...] * column(out_gain[...], 384) + column(out_bias[...], 384)
    proj = dot(w_out[...], inner_n.astype(BF16), (0, 0))
    sig = out_sig[...]
    store_tile((sig * proj).T, tile, update)
    d_gate_out = (upstream[...] * proj * sig * (1.0 - sig)).astype(BF16)
    d_normed[...] = dot(d_gate_out, w_out_gate[...], (0, 1))


def grad_kernel(d_inner, left, right, d_left, d_right, rows, matrix):
    rows[...] = d_inner[...].astype(F32)
    to_matrix(rows, 0, 4, matrix)
    packed = dot(matrix[...].astype(BF16), spread(), (1, 1)).astype(BF16)
    d_left[...] = dot(packed, right[...].reshape(384, 384), (1, 0)).astype(BF16)
    d_right[...] = dot(packed, left[...], (0, 0)).astype(BF16).reshape(4, 96, 384)


def merge_kernel(d_left, d_right, d_both, rows):
    one_hot = spread()
    to_rows(dot(d_left[...], one_hot, (1, 0)), rows, 0, 8)
    parts = [d_right[part].astype(F32) for part in range(4)]
    total = ((parts[0] + parts[1]) + (parts[2] + parts[3])).astype(BF16)
    to_rows(dot(total, one_hot, (1, 0)), rows, 3, 8)
    for spare in (6, 7):
        rows[pl.ds(spare, 128, stride=8), :] = jnp.zeros((128, 128), F32)
    d_both[...] = rows[...].astype(BF16)


def back_kernel(counts, d_both, values, gate, d_out, hat, inv, gain, w_values, w_gates, grad, rows, tile):
    rows[...] = d_both[...].astype(F32)
    parts = [
        jnp.concatenate([rows[pl.ds(3 * side + i_hi, 128, stride=8), :] for i_hi in range(3)], axis=1)
        for side in range(2)
    ]
    incoming = jnp.concatenate(parts, axis=0) * live_mask(counts)
    sig = gate[...]
    d_values = (incoming * sig).astype(BF16)
    d_gates = (incoming * values[...] * sig * (1.0 - sig)).astype(BF16)
    d_normed = d_out[...] + dot(d_values, w_values[...], (0, 1)) + dot(d_gates, w_gates[...], (0, 1))
    scaled = d_normed * gain[...].reshape(1, 128)
    pair_hat = hat[...]
    first_mean = jnp.mean(scaled, axis=1, keepdims=True)
    second_mean = jnp.mean(scaled * pair_hat, axis=1, keepdims=True)
    store_tile(inv[...] * (scaled - first_mean - pair_hat * second_mean), tile, grad)


def call(kernel, outs, args, scratch=(), scalars=0, flops=0):
    vmem, smem = pl.BlockSpec(memory_space=pltpu.VMEM), pl.BlockSpec(memory_space=pltpu.SMEM)
    outs = [jax.ShapeDtypeStruct(shape, dtype) for shape, dtype in outs]
    size = sum(a.size * a.dtype.itemsize for a in list(args) + outs)
    return pl.pallas_call(
        kernel,
        out_shape=outs,
        in_specs=[smem] * scalars + [vmem] * (len(args) - scalars),
        out_specs=[vmem] * len(outs),
        scratch_shapes=[pltpu.VMEM(shape, F32) for shape in scratch],
        compiler_params=pltpu.CompilerParams(vmem_limit_bytes=24 * 1024 * 1024),
        cost_estimate=pl.CostEstimate(flops=flops, bytes_accessed=size, transcendentals=0),
    )(*args)


def exchange(rows):
    return lax.all_to_all(rows.reshape(128, -1, 128), GROUP, 0, 0).reshape(rows.shape)


def shards(
    pair,
    cotangent,
    chain_counts,
    in_gain,
    in_bias,
    w_values,
    w_gates,
    w_out_gate,
    out_gain,
    out_bias,
    w_out,
):
    pair, cotangent = pair.transpose(1, 0, 2), cotangent.transpose(1, 0, 2)
    wide, tall, tokens, tile = (256, 384), (128, 384), (384, 128), (12, 24, 128)
    one, two = (512, 128), (1024, 128)
    both, values, gate, hat, inv, normed = call(
        front_kernel,
        [(two, BF16), (wide, F32), (wide, F32), (tokens, F32), (tokens, F32), (tokens, BF16)],
        [chain_counts, pair, in_gain, in_bias, w_values, w_gates],
        [two],
        scalars=1,
    )
    both = exchange(both)
    out_sig, upstream, scaled = call(
        gate_kernel, [(tall, F32)] * 3, [normed, cotangent, w_out_gate, w_out, out_gain]
    )
    left, right = call(split_kernel, [((96, 384), BF16), ((4, 96, 384), BF16)], [both], [two, (96, 512)])
    right = lax.all_to_all(right, "x", 0, 0)
    (inner,) = call(inner_kernel, [(one, BF16)], [left, right], [one])
    inner = exchange(inner)
    d_inner, inner_hat = call(norm_kernel, [(one, BF16), (tall, F32)], [inner, scaled], [one])
    d_inner = exchange(d_inner)
    update, d_out = call(
        update_kernel,
        [(tile, BF16), (tokens, F32)],
        [inner_hat, out_sig, upstream, out_gain, out_bias, w_out, w_out_gate],
        [tile],
    )
    d_left, d_right = call(
        grad_kernel, [((96, 384), BF16), ((4, 96, 384), BF16)], [d_inner, left, right], [one, (96, 512)]
    )
    d_right = lax.all_to_all(d_right, "x", 0, 0)
    (d_both,) = call(merge_kernel, [(two, BF16)], [d_left, d_right], [two])
    d_both = exchange(d_both)
    (grad,) = call(
        back_kernel,
        [(tile, BF16)],
        [chain_counts, d_both, values, gate, d_out, hat, inv, in_gain, w_values, w_gates],
        [two, tile],
        scalars=1,
    )
    return (update.transpose(1, 0, 2), grad.transpose(1, 0, 2))


def solution(mesh):
    fine = Mesh(mesh.devices.reshape(4, 4, 8, 2, 2), ROW + COL)
    placed = P(ROW, COL, None)
    return jax.shard_map(
        shards,
        mesh=fine,
        in_specs=(placed, placed) + (P(),) * 9,
        out_specs=(placed, placed),
        check_vma=False,
    )
```

```python
import jax
import jax.numpy as jnp
from jax import lax
from jax.experimental import pallas as pl
from jax.experimental.pallas import tpu as pltpu
from jax.sharding import Mesh
from jax.sharding import PartitionSpec as P

EPS = 1e-05
F32 = jnp.float32
BF16 = jnp.bfloat16
ROW = ("x", "z_lo")
COL = ("y", "z_hi", "core")
GROUP = ("z_lo",) + COL
SLOTS = 16
LOW = 8


def dot(a, b, contract):
    return lax.dot_general(a, b, ((contract[:1], contract[1:]), ((), ())), preferred_element_type=F32)


def swap_groups(x):
    sub = lax.broadcasted_iota(jnp.int32, x.shape, 1)
    lane = lax.broadcasted_iota(jnp.int32, x.shape, 2)
    for step in (4, 2, 1):
        up = pltpu.roll(pltpu.roll(x, LOW - step, 1), step, 2)
        down = pltpu.roll(pltpu.roll(x, step, 1), 128 - step, 2)
        sub_bit, lane_bit = (sub & step) != 0, (lane & step) != 0
        x = jnp.where(sub_bit == lane_bit, x, jnp.where(lane_bit, up, down))
    return x


def to_matrix(rows, first, per, out):
    for i_hi in range(3):
        part = rows[pl.ds(first + i_hi, 128, stride=per), :].reshape(16, LOW, 128)
        part = swap_groups(part)
        for z in range(4):
            for c_hi in range(4):
                row = 24 * z + LOW * i_hi
                out[row : row + LOW, 128 * c_hi : 128 * (c_hi + 1)] = part[4 * z + c_hi]


def to_rows(matrix, rows, first, per):
    for i_hi in range(3):
        parts = []
        for z in range(4):
            row = 24 * z + LOW * i_hi
            parts += [matrix[row : row + LOW, 128 * c : 128 * (c + 1)] for c in range(4)]
        rows[pl.ds(first + i_hi, 128, stride=per), :] = swap_groups(jnp.stack(parts)).reshape(128, 128)


def spread():
    lane = lax.broadcasted_iota(jnp.int32, (1, 512), 1)
    slot = lane % 128 // LOW
    token = (lane // 128 * LOW + lane % LOW) * 12 + slot
    token = jnp.where(slot < 12, token, -1)
    hit = lax.broadcasted_iota(jnp.int32, (384, 512), 0) == token
    return jnp.where(hit, 1.0, 0.0).astype(BF16)


def live_mask(counts):
    valid = counts[0] + counts[1] + counts[2] + counts[3]
    lane = lax.broadcasted_iota(jnp.int32, (1, 384), 1)
    i, j = lane // 128 * LOW + lane % LOW, lane % 128 // LOW
    row = lax.axis_index("x") * 4 + lax.axis_index("z_lo")
    col = lax.axis_index("y") * 4 + lax.axis_index("z_hi") * 2 + lax.axis_index("core")
    live = (row * 24 + i < valid) & (col * 12 + j < valid) & (j < 12)
    return live.astype(F32)


def column(vector, width):
    square = jnp.broadcast_to(vector.reshape(1, 128), (128, 128)).T
    return jnp.concatenate([square] * (width // 128), axis=1)


def load_tile(tile):
    x = tile[...].astype(F32)
    gap = jnp.zeros(((SLOTS - 12) * LOW, 128), F32)
    parts = []
    for i_hi in range(3):
        parts += [x[:, LOW * i_hi : LOW * (i_hi + 1)].reshape(12 * LOW, 128), gap]
    return jnp.concatenate(parts, axis=0)


def store_tile(value, scratch, tile):
    for i_hi in range(3):
        part = value[128 * i_hi : 128 * i_hi + 12 * LOW].reshape(12, LOW, 128)
        scratch[:, LOW * i_hi : LOW * (i_hi + 1), :] = part
    tile[...] = scratch[...].astype(BF16)


def third(value, i_hi):
    return value[:, 128 * i_hi : 128 * (i_hi + 1)]


def front_kernel(
    counts, pair, gain, bias, w_values, w_gates, both, values, gate, hat, inv, normed,
    rows, counts_s, pair_s, gain_s, bias_s, w_values_s, w_gates_s, sems,
):
    ends = ((pair, pair_s), (gain, gain_s), (bias, bias_s), (w_values, w_values_s), (w_gates, w_gates_s), (counts, counts_s))
    copies = [pltpu.make_async_copy(src, dst, sems.at[n]) for n, (src, dst) in enumerate(ends)]
    for copy in copies:
        copy.start()
    copies[0].wait()
    x = load_tile(pair_s)
    centre = x - jnp.mean(x, axis=1, keepdims=True)
    inv_std = lax.rsqrt(jnp.mean(centre * centre, axis=1, keepdims=True) + EPS)
    pair_hat = centre * inv_std
    for copy in copies[1:]:
        copy.wait()
    normed_b = (pair_hat * gain_s[...] + bias_s[...]).astype(BF16)
    hat[...] = pair_hat
    inv[...] = jnp.broadcast_to(inv_std, (384, 128))
    normed[...] = normed_b
    vals = dot(w_values_s[...], normed_b, (0, 1))
    sig = jax.nn.sigmoid(dot(w_gates_s[...], normed_b, (0, 1)))
    values[...] = vals
    gate[...] = sig
    out = sig * vals * live_mask(counts_s)
    for i_hi in range(3):
        rows[pl.ds(i_hi, 128, stride=8), :] = third(out[:128], i_hi)
        rows[pl.ds(3 + i_hi, 128, stride=8), :] = third(out[128:], i_hi)
    for spare in (6, 7):
        rows[pl.ds(spare, 128, stride=8), :] = jnp.zeros((128, 128), F32)
    both[...] = rows[...].astype(BF16)


def gate_kernel(
    counts, normed, cotangent, values, gate, hat, inv, w_out_gate, w_out, in_gain, out_gain,
    out_sig, upstream, scaled, to_values, to_gates, hat_t, inv_t, gain_t,
):
    sig = jax.nn.sigmoid(dot(w_out_gate[...], normed[...], (0, 1)))
    up = load_tile(cotangent).T
    d_proj = (up * sig).astype(BF16)
    out_sig[...] = sig
    upstream[...] = up
    scaled[...] = dot(w_out[...], d_proj, (1, 0)) * column(out_gain[...], 384)
    live = live_mask(counts)
    sig = gate[...]
    to_values[...] = sig * live
    to_gates[...] = values[...] * sig * (1.0 - sig) * live
    hat_t[...] = hat[...].T
    inv_t[...] = inv[...].T[:8]
    gain_t[...] = column(in_gain[...], 128)


def split_kernel(both, left, right, rows, matrix):
    rows[...] = both[...].astype(F32)
    one_hot = spread()
    to_matrix(rows, 0, 8, matrix)
    left[...] = dot(matrix[...].astype(BF16), one_hot, (1, 1)).astype(BF16)
    to_matrix(rows, 3, 8, matrix)
    packed = dot(matrix[...].astype(BF16), one_hot, (1, 1)).astype(BF16)
    for part in range(4):
        right[part] = packed


def inner_kernel(left, right, inner, rows):
    product = dot(left[...], right[...].reshape(384, 384), (1, 1)).astype(BF16)
    to_rows(dot(product, spread(), (1, 0)), rows, 0, 4)
    rows[pl.ds(3, 128, stride=4), :] = jnp.zeros((128, 128), F32)
    inner[...] = rows[...].astype(BF16)


def norm_kernel(inner, scaled, d_inner, inner_hat, rows):
    rows[...] = inner[...].astype(F32)
    for i_hi in range(3):
        x = rows[pl.ds(i_hi, 128, stride=4), :]
        centre = x - jnp.mean(x, axis=0, keepdims=True)
        inv_std = lax.rsqrt(jnp.mean(centre * centre, axis=0, keepdims=True) + EPS)
        hat = centre * inv_std
        up = scaled[:, 128 * i_hi : 128 * (i_hi + 1)]
        first_mean = jnp.mean(up, axis=0, keepdims=True)
        second_mean = jnp.mean(up * hat, axis=0, keepdims=True)
        rows[pl.ds(i_hi, 128, stride=4), :] = inv_std * (up - first_mean - hat * second_mean)
        inner_hat[:, 128 * i_hi : 128 * (i_hi + 1)] = hat
    d_inner[...] = rows[...].astype(BF16)


def update_kernel(inner_hat, out_sig, upstream, out_gain, out_bias, w_out, w_out_gate, update, d_normed, tile):
    inner_n = inner_hat[...] * column(out_gain[...], 384) + column(out_bias[...], 384)
    proj = dot(w_out[...], inner_n.astype(BF16), (0, 0))
    sig = out_sig[...]
    store_tile((sig * proj).T, tile, update)
    d_gate_out = (upstream[...] * proj * sig * (1.0 - sig)).astype(BF16)
    d_normed[...] = dot(w_out_gate[...], d_gate_out, (1, 0))


def grad_kernel(d_inner, left, right, d_left, d_right, rows, matrix):
    rows[...] = d_inner[...].astype(F32)
    to_matrix(rows, 0, 4, matrix)
    packed = dot(matrix[...].astype(BF16), spread(), (1, 1)).astype(BF16)
    d_left[...] = dot(packed, right[...].reshape(384, 384), (1, 0)).astype(BF16)
    d_right[...] = dot(packed, left[...], (0, 0)).astype(BF16).reshape(4, 96, 384)


def merge_kernel(d_left, d_right, d_both, rows):
    one_hot = spread()
    to_rows(dot(d_left[...], one_hot, (1, 0)), rows, 0, 8)
    parts = [d_right[part].astype(F32) for part in range(4)]
    total = ((parts[0] + parts[1]) + (parts[2] + parts[3])).astype(BF16)
    to_rows(dot(total, one_hot, (1, 0)), rows, 3, 8)
    for spare in (6, 7):
        rows[pl.ds(spare, 128, stride=8), :] = jnp.zeros((128, 128), F32)
    d_both[...] = rows[...].astype(BF16)


def back_kernel(d_both, to_values, to_gates, d_out, hat_t, inv_t, gain_t, w_values, w_gates, grad, rows, tile):
    rows[...] = d_both[...].astype(F32)
    parts = [
        jnp.concatenate([rows[pl.ds(3 * side + i_hi, 128, stride=8), :] for i_hi in range(3)], axis=1)
        for side in range(2)
    ]
    incoming = jnp.concatenate(parts, axis=0)
    d_values = (incoming * to_values[...]).astype(BF16)
    d_gates = (incoming * to_gates[...]).astype(BF16)
    d_normed = d_out[...] + dot(w_values[...], d_values, (1, 0)) + dot(w_gates[...], d_gates, (1, 0))
    scaled = d_normed * jnp.concatenate([gain_t[...]] * 3, axis=1)
    pair_hat = hat_t[...]
    first_mean = jnp.mean(scaled, axis=0, keepdims=True)
    second_mean = jnp.mean(scaled * pair_hat, axis=0, keepdims=True)
    store_tile((inv_t[:1] * (scaled - first_mean - pair_hat * second_mean)).T, tile, grad)


def call(kernel, outs, args, scratch=(), scalars=0, flops=0, last=0):
    vmem, smem = pl.BlockSpec(memory_space=pltpu.VMEM), pl.BlockSpec(memory_space=pltpu.SMEM)
    size = sum(a.size * a.dtype.itemsize for a in args)
    shapes = [jax.ShapeDtypeStruct(*out) if n < last else pltpu.VMEM(*out) for n, out in enumerate(outs)]
    return pl.pallas_call(
        kernel,
        out_shape=shapes,
        in_specs=[smem] * scalars + [vmem] * (len(args) - scalars),
        out_specs=[vmem] * len(outs),
        scratch_shapes=[pltpu.VMEM(shape, F32) for shape in scratch],
        compiler_params=pltpu.CompilerParams(vmem_limit_bytes=24 * 1024 * 1024),
        cost_estimate=pl.CostEstimate(flops=flops, bytes_accessed=size, transcendentals=0),
    )(*args)


def call_front(outs, args, rows):
    args = [pltpu.with_memory_space_constraint(arg, pltpu.HBM) for arg in args]
    spaces = [pltpu.SMEM] + [pltpu.VMEM] * 5
    held = [space(arg.shape, arg.dtype) for space, arg in zip(spaces, args)]
    return pl.pallas_call(
        front_kernel,
        out_shape=[pltpu.VMEM(*out) for out in outs],
        in_specs=[pl.BlockSpec(memory_space=pltpu.HBM)] * 6,
        out_specs=[pl.BlockSpec(memory_space=pltpu.VMEM)] * len(outs),
        scratch_shapes=[pltpu.VMEM(rows, F32)] + held + [pltpu.SemaphoreType.DMA((6,))],
        compiler_params=pltpu.CompilerParams(vmem_limit_bytes=24 * 1024 * 1024),
    )(*args)


def exchange(rows):
    return lax.all_to_all(rows.reshape(128, -1, 128), GROUP, 0, 0).reshape(rows.shape)


def shards(
    pair,
    cotangent,
    chain_counts,
    in_gain,
    in_bias,
    w_values,
    w_gates,
    w_out_gate,
    out_gain,
    out_bias,
    w_out,
):
    pair, cotangent = pair.transpose(1, 0, 2), cotangent.transpose(1, 0, 2)
    wide, tall, tokens, tile = (256, 384), (128, 384), (384, 128), (12, 24, 128)
    one, two = (512, 128), (1024, 128)
    both, values, gate, hat, inv, normed = call_front(
        [(two, BF16), (wide, F32), (wide, F32), (tokens, F32), (tokens, F32), (tokens, BF16)],
        [chain_counts, pair, in_gain.reshape(1, 128), in_bias.reshape(1, 128), w_values, w_gates],
        two,
    )
    both = exchange(both)
    out_sig, upstream, scaled, to_values, to_gates, hat_t, inv_t, gain_t = call(
        gate_kernel,
        [(tall, F32)] * 3 + [(wide, F32)] * 2 + [(tall, F32), ((8, 384), F32), ((128, 128), F32)],
        [chain_counts, normed, cotangent, values, gate, hat, inv, w_out_gate, w_out, in_gain, out_gain],
        scalars=1,
    )
    left, right = call(split_kernel, [((96, 384), BF16), ((4, 96, 384), BF16)], [both], [two, (96, 512)])
    right = lax.all_to_all(right, "x", 0, 0)
    (inner,) = call(inner_kernel, [(one, BF16)], [left, right], [one])
    inner = exchange(inner)
    d_inner, inner_hat = call(norm_kernel, [(one, BF16), (tall, F32)], [inner, scaled], [one])
    d_inner = exchange(d_inner)
    update, d_out = call(
        update_kernel,
        [(tile, BF16), (tall, F32)],
        [inner_hat, out_sig, upstream, out_gain, out_bias, w_out, w_out_gate],
        [tile],
        last=1,
    )
    d_left, d_right = call(
        grad_kernel, [((96, 384), BF16), ((4, 96, 384), BF16)], [d_inner, left, right], [one, (96, 512)]
    )
    d_right = lax.all_to_all(d_right, "x", 0, 0)
    (d_both,) = call(merge_kernel, [(two, BF16)], [d_left, d_right], [two])
    d_both = exchange(d_both)
    (grad,) = call(
        back_kernel,
        [(tile, BF16)],
        [d_both, to_values, to_gates, d_out, hat_t, inv_t, gain_t, w_values, w_gates],
        [two, tile],
        last=1,
    )
    return (update.transpose(1, 0, 2), grad.transpose(1, 0, 2))


def solution(mesh):
    fine = Mesh(mesh.devices.reshape(4, 4, 8, 2, 2), ROW + COL)
    placed = P(ROW, COL, None)
    return jax.shard_map(
        shards,
        mesh=fine,
        in_specs=(placed, placed) + (P(),) * 9,
        out_specs=(placed, placed),
        check_vma=False,
    )
```

```python
import jax
import jax.numpy as jnp
from jax import lax
from jax.experimental import pallas as pl
from jax.experimental.pallas import tpu as pltpu
from jax.sharding import Mesh
from jax.sharding import PartitionSpec as P

EPS = 1e-05
F32 = jnp.float32
BF16 = jnp.bfloat16
ROW = ("x", "z_lo")
COL = ("y", "z_hi", "core")
GROUP = ("z_lo",) + COL
SLOTS = 16
LOW = 8


def dot(a, b, contract):
    return lax.dot_general(a, b, ((contract[:1], contract[1:]), ((), ())), preferred_element_type=F32)


def swap_groups(x):
    sub = lax.broadcasted_iota(jnp.int32, x.shape, 1)
    lane = lax.broadcasted_iota(jnp.int32, x.shape, 2)
    for step in (4, 2, 1):
        up = pltpu.roll(pltpu.roll(x, LOW - step, 1), step, 2)
        down = pltpu.roll(pltpu.roll(x, step, 1), 128 - step, 2)
        sub_bit, lane_bit = (sub & step) != 0, (lane & step) != 0
        x = jnp.where(sub_bit == lane_bit, x, jnp.where(lane_bit, up, down))
    return x


def to_matrix(rows, first, per, out):
    for i_hi in range(3):
        part = rows[pl.ds(first + i_hi, 128, stride=per), :].reshape(16, LOW, 128)
        part = swap_groups(part)
        for z in range(4):
            for c_hi in range(4):
                row = 24 * z + LOW * i_hi
                out[row : row + LOW, 128 * c_hi : 128 * (c_hi + 1)] = part[4 * z + c_hi]


def to_rows(matrix, rows, first, per):
    for i_hi in range(3):
        parts = []
        for z in range(4):
            row = 24 * z + LOW * i_hi
            parts += [matrix[row : row + LOW, 128 * c : 128 * (c + 1)] for c in range(4)]
        rows[pl.ds(first + i_hi, 128, stride=per), :] = swap_groups(jnp.stack(parts)).reshape(128, 128)


def spread():
    lane = lax.broadcasted_iota(jnp.int32, (1, 512), 1)
    slot = lane % 128 // LOW
    token = (lane // 128 * LOW + lane % LOW) * 12 + slot
    token = jnp.where(slot < 12, token, -1)
    hit = lax.broadcasted_iota(jnp.int32, (384, 512), 0) == token
    return jnp.where(hit, 1.0, 0.0).astype(BF16)


def live_mask(counts):
    valid = counts[0] + counts[1] + counts[2] + counts[3]
    lane = lax.broadcasted_iota(jnp.int32, (1, 384), 1)
    i, j = lane // 128 * LOW + lane % LOW, lane % 128 // LOW
    row = lax.axis_index("x") * 4 + lax.axis_index("z_lo")
    col = lax.axis_index("y") * 4 + lax.axis_index("z_hi") * 2 + lax.axis_index("core")
    live = (row * 24 + i < valid) & (col * 12 + j < valid) & (j < 12)
    return live.astype(F32)


def column(vector, width):
    square = jnp.broadcast_to(vector.reshape(1, 128), (128, 128)).T
    return jnp.concatenate([square] * (width // 128), axis=1)


def load_tile(tile):
    x = tile[...].astype(F32)
    gap = jnp.zeros(((SLOTS - 12) * LOW, 128), F32)
    parts = []
    for i_hi in range(3):
        parts += [x[:, LOW * i_hi : LOW * (i_hi + 1)].reshape(12 * LOW, 128), gap]
    return jnp.concatenate(parts, axis=0)


def store_tile(value, scratch, tile):
    for i_hi in range(3):
        part = value[128 * i_hi : 128 * i_hi + 12 * LOW].reshape(12, LOW, 128)
        scratch[:, LOW * i_hi : LOW * (i_hi + 1), :] = part
    tile[...] = scratch[...].astype(BF16)


def third(value, i_hi):
    return value[:, 128 * i_hi : 128 * (i_hi + 1)]


def front_kernel(
    counts, pair, gain, bias, w_values, w_gates, both, values, gate, hat, inv, normed,
    rows, counts_s, pair_s, gain_s, bias_s, w_values_s, w_gates_s, sems,
):
    ends = ((pair, pair_s), (gain, gain_s), (bias, bias_s), (w_values, w_values_s), (w_gates, w_gates_s), (counts, counts_s))
    copies = [pltpu.make_async_copy(src, dst, sems.at[n]) for n, (src, dst) in enumerate(ends)]
    for copy in copies:
        copy.start()
    copies[0].wait()
    x = load_tile(pair_s)
    centre = x - jnp.mean(x, axis=1, keepdims=True)
    inv_std = lax.rsqrt(jnp.mean(centre * centre, axis=1, keepdims=True) + EPS)
    pair_hat = centre * inv_std
    for copy in copies[1:]:
        copy.wait()
    normed_b = (pair_hat * gain_s[...] + bias_s[...]).astype(BF16)
    hat[...] = pair_hat
    inv[...] = jnp.broadcast_to(inv_std, (384, 128))
    normed[...] = normed_b
    vals = dot(w_values_s[...], normed_b, (0, 1))
    sig = jax.nn.sigmoid(dot(w_gates_s[...], normed_b, (0, 1)))
    values[...] = vals
    gate[...] = sig
    out = sig * vals * live_mask(counts_s)
    for i_hi in range(3):
        rows[pl.ds(i_hi, 128, stride=6), :] = third(out[:128], i_hi)
        rows[pl.ds(3 + i_hi, 128, stride=6), :] = third(out[128:], i_hi)
    both[...] = rows[...].astype(BF16)


def gate_kernel(
    counts, normed, cotangent, values, gate, hat, inv, w_out_gate, w_out, in_gain, out_gain,
    out_sig, upstream, scaled, to_values, to_gates, hat_t, inv_t, gain_t,
):
    sig = jax.nn.sigmoid(dot(w_out_gate[...], normed[...], (0, 1)))
    up = load_tile(cotangent).T
    d_proj = (up * sig).astype(BF16)
    out_sig[...] = sig
    upstream[...] = up
    scaled[...] = dot(w_out[...], d_proj, (1, 0)) * column(out_gain[...], 384)
    live = live_mask(counts)
    sig = gate[...]
    to_values[...] = sig * live
    to_gates[...] = values[...] * sig * (1.0 - sig) * live
    hat_t[...] = hat[...].T
    inv_t[...] = inv[...].T[:8]
    gain_t[...] = column(in_gain[...], 128)


def split_kernel(both, left, right, rows, matrix):
    rows[...] = both[...].astype(F32)
    one_hot = spread()
    to_matrix(rows, 0, 6, matrix)
    left[...] = dot(matrix[...].astype(BF16), one_hot, (1, 1)).astype(BF16)
    to_matrix(rows, 3, 6, matrix)
    packed = dot(matrix[...].astype(BF16), one_hot, (1, 1)).astype(BF16)
    for part in range(4):
        right[part] = packed


def inner_kernel(left, right, inner, rows):
    product = dot(left[...], right[...].reshape(384, 384), (1, 1)).astype(BF16)
    to_rows(dot(product, spread(), (1, 0)), rows, 0, 4)
    rows[pl.ds(3, 128, stride=4), :] = jnp.zeros((128, 128), F32)
    inner[...] = rows[...].astype(BF16)


def norm_kernel(inner, scaled, d_inner, inner_hat, rows):
    rows[...] = inner[...].astype(F32)
    for i_hi in range(3):
        x = rows[pl.ds(i_hi, 128, stride=4), :]
        centre = x - jnp.mean(x, axis=0, keepdims=True)
        inv_std = lax.rsqrt(jnp.mean(centre * centre, axis=0, keepdims=True) + EPS)
        hat = centre * inv_std
        up = scaled[:, 128 * i_hi : 128 * (i_hi + 1)]
        first_mean = jnp.mean(up, axis=0, keepdims=True)
        second_mean = jnp.mean(up * hat, axis=0, keepdims=True)
        rows[pl.ds(i_hi, 128, stride=4), :] = inv_std * (up - first_mean - hat * second_mean)
        inner_hat[:, 128 * i_hi : 128 * (i_hi + 1)] = hat
    d_inner[...] = rows[...].astype(BF16)


def update_kernel(inner_hat, out_sig, upstream, out_gain, out_bias, w_out, w_out_gate, update, d_normed, tile):
    inner_n = inner_hat[...] * column(out_gain[...], 384) + column(out_bias[...], 384)
    proj = dot(w_out[...], inner_n.astype(BF16), (0, 0))
    sig = out_sig[...]
    store_tile((sig * proj).T, tile, update)
    d_gate_out = (upstream[...] * proj * sig * (1.0 - sig)).astype(BF16)
    d_normed[...] = dot(w_out_gate[...], d_gate_out, (1, 0))


def grad_kernel(d_inner, left, right, d_left, d_right, rows, matrix):
    rows[...] = d_inner[...].astype(F32)
    to_matrix(rows, 0, 4, matrix)
    packed = dot(matrix[...].astype(BF16), spread(), (1, 1)).astype(BF16)
    d_left[...] = dot(packed, right[...].reshape(384, 384), (1, 0)).astype(BF16)
    d_right[...] = dot(packed, left[...], (0, 0)).astype(BF16).reshape(4, 96, 384)


def merge_kernel(d_left, d_right, d_both, rows):
    one_hot = spread()
    to_rows(dot(d_left[...], one_hot, (1, 0)), rows, 0, 6)
    parts = [d_right[part].astype(F32) for part in range(4)]
    total = ((parts[0] + parts[1]) + (parts[2] + parts[3])).astype(BF16)
    to_rows(dot(total, one_hot, (1, 0)), rows, 3, 6)
    d_both[...] = rows[...].astype(BF16)


def back_kernel(d_both, to_values, to_gates, d_out, hat_t, inv_t, gain_t, w_values, w_gates, grad, rows, tile):
    rows[...] = d_both[...].astype(F32)
    parts = [
        jnp.concatenate([rows[pl.ds(3 * side + i_hi, 128, stride=6), :] for i_hi in range(3)], axis=1)
        for side in range(2)
    ]
    incoming = jnp.concatenate(parts, axis=0)
    d_values = (incoming * to_values[...]).astype(BF16)
    d_gates = (incoming * to_gates[...]).astype(BF16)
    d_normed = d_out[...] + dot(w_values[...], d_values, (1, 0)) + dot(w_gates[...], d_gates, (1, 0))
    scaled = d_normed * jnp.concatenate([gain_t[...]] * 3, axis=1)
    pair_hat = hat_t[...]
    first_mean = jnp.mean(scaled, axis=0, keepdims=True)
    second_mean = jnp.mean(scaled * pair_hat, axis=0, keepdims=True)
    store_tile((inv_t[:1] * (scaled - first_mean - pair_hat * second_mean)).T, tile, grad)


def call(kernel, outs, args, scratch=(), scalars=0, flops=0, last=0):
    vmem, smem = pl.BlockSpec(memory_space=pltpu.VMEM), pl.BlockSpec(memory_space=pltpu.SMEM)
    size = sum(a.size * a.dtype.itemsize for a in args)
    shapes = [jax.ShapeDtypeStruct(*out) if n < last else pltpu.VMEM(*out) for n, out in enumerate(outs)]
    return pl.pallas_call(
        kernel,
        out_shape=shapes,
        in_specs=[smem] * scalars + [vmem] * (len(args) - scalars),
        out_specs=[vmem] * len(outs),
        scratch_shapes=[pltpu.VMEM(shape, F32) for shape in scratch],
        compiler_params=pltpu.CompilerParams(vmem_limit_bytes=24 * 1024 * 1024),
        cost_estimate=pl.CostEstimate(flops=flops, bytes_accessed=size, transcendentals=0),
    )(*args)


def call_front(outs, args, rows):
    args = [pltpu.with_memory_space_constraint(arg, pltpu.HBM) for arg in args]
    spaces = [pltpu.SMEM] + [pltpu.VMEM] * 5
    held = [space(arg.shape, arg.dtype) for space, arg in zip(spaces, args)]
    return pl.pallas_call(
        front_kernel,
        out_shape=[pltpu.VMEM(*out) for out in outs],
        in_specs=[pl.BlockSpec(memory_space=pltpu.HBM)] * 6,
        out_specs=[pl.BlockSpec(memory_space=pltpu.VMEM)] * len(outs),
        scratch_shapes=[pltpu.VMEM(rows, F32)] + held + [pltpu.SemaphoreType.DMA((6,))],
        compiler_params=pltpu.CompilerParams(vmem_limit_bytes=24 * 1024 * 1024),
    )(*args)


def exchange(rows):
    return lax.all_to_all(rows.reshape(128, -1, 2, 128), GROUP, 0, 0).reshape(rows.shape)


def shards(
    pair,
    cotangent,
    chain_counts,
    in_gain,
    in_bias,
    w_values,
    w_gates,
    w_out_gate,
    out_gain,
    out_bias,
    w_out,
):
    pair, cotangent = pair.transpose(1, 0, 2), cotangent.transpose(1, 0, 2)
    wide, tall, tokens, tile = (256, 384), (128, 384), (384, 128), (12, 24, 128)
    one, two = (512, 128), (768, 128)
    both, values, gate, hat, inv, normed = call_front(
        [(two, BF16), (wide, F32), (wide, F32), (tokens, F32), (tokens, F32), (tokens, BF16)],
        [chain_counts, pair, in_gain.reshape(1, 128), in_bias.reshape(1, 128), w_values, w_gates],
        two,
    )
    both = exchange(both)
    out_sig, upstream, scaled, to_values, to_gates, hat_t, inv_t, gain_t = call(
        gate_kernel,
        [(tall, F32)] * 3 + [(wide, F32)] * 2 + [(tall, F32), ((8, 384), F32), ((128, 128), F32)],
        [chain_counts, normed, cotangent, values, gate, hat, inv, w_out_gate, w_out, in_gain, out_gain],
        scalars=1,
    )
    left, right = call(split_kernel, [((96, 384), BF16), ((4, 96, 384), BF16)], [both], [two, (96, 512)])
    right = lax.all_to_all(right, "x", 0, 0)
    (inner,) = call(inner_kernel, [(one, BF16)], [left, right], [one])
    inner = exchange(inner)
    d_inner, inner_hat = call(norm_kernel, [(one, BF16), (tall, F32)], [inner, scaled], [one])
    d_inner = exchange(d_inner)
    update, d_out = call(
        update_kernel,
        [(tile, BF16), (tall, F32)],
        [inner_hat, out_sig, upstream, out_gain, out_bias, w_out, w_out_gate],
        [tile],
        last=1,
    )
    d_left, d_right = call(
        grad_kernel, [((96, 384), BF16), ((4, 96, 384), BF16)], [d_inner, left, right], [one, (96, 512)]
    )
    d_right = lax.all_to_all(d_right, "x", 0, 0)
    (d_both,) = call(merge_kernel, [(two, BF16)], [d_left, d_right], [two])
    d_both = exchange(d_both)
    (grad,) = call(
        back_kernel,
        [(tile, BF16)],
        [d_both, to_values, to_gates, d_out, hat_t, inv_t, gain_t, w_values, w_gates],
        [two, tile],
        last=1,
    )
    return (update.transpose(1, 0, 2), grad.transpose(1, 0, 2))


def solution(mesh):
    fine = Mesh(mesh.devices.reshape(4, 4, 8, 2, 2), ROW + COL)
    placed = P(ROW, COL, None)
    return jax.shard_map(
        shards,
        mesh=fine,
        in_specs=(placed, placed) + (P(),) * 9,
        out_specs=(placed, placed),
        check_vma=False,
    )
```

```python
import jax
import jax.numpy as jnp
from jax import lax
from jax.experimental import pallas as pl
from jax.experimental.pallas import tpu as pltpu
from jax.sharding import Mesh
from jax.sharding import PartitionSpec as P

EPS = 1e-05
F32 = jnp.float32
BF16 = jnp.bfloat16
ROW = ("x", "z_lo")
COL = ("y", "z_hi", "core")
GROUP = ("z_lo",) + COL
SLOTS = 16
LOW = 8


def dot(a, b, contract):
    return lax.dot_general(a, b, ((contract[:1], contract[1:]), ((), ())), preferred_element_type=F32)


def swap_quads(quad):
    lane = lax.broadcasted_iota(jnp.int32, (LOW, 128), 1)
    quad = list(quad)
    for step in (2, 1):
        low = (lane & (32 * step)) == 0
        for a in range(4):
            if a & step == 0:
                one, two = quad[a], quad[a + step]
                quad[a] = jnp.where(low, one, pltpu.roll(two, 32 * step, 1))
                quad[a + step] = jnp.where(low, pltpu.roll(one, 128 - 32 * step, 1), two)
    return quad


def to_matrix(rows, first, per):
    bands = {}
    for i_hi in range(3):
        turned = rows[pl.ds(first + i_hi, 128, stride=per), :].T
        for j_hi in range(3):
            parts = [turned[LOW * (4 * j_hi + j_lo) : LOW * (4 * j_hi + j_lo + 1)] for j_lo in range(4)]
            for z, part in enumerate(swap_quads(parts)):
                bands[z, i_hi, j_hi] = part
    return jnp.concatenate(
        [
            jnp.concatenate([bands[z, i_hi, j_hi] for j_hi in range(3)], axis=1)
            for z in range(4)
            for i_hi in range(3)
        ],
        axis=0,
    )


def to_rows(matrix, rows, first, per):
    for i_hi in range(3):
        parts = []
        for j_hi in range(3):
            bands = [24 * z + LOW * i_hi for z in range(4)]
            parts += swap_quads([matrix[band : band + LOW, 128 * j_hi : 128 * (j_hi + 1)] for band in bands])
        parts += [jnp.zeros(((SLOTS - 12) * LOW, 128), F32)]
        rows[pl.ds(first + i_hi, 128, stride=per), :] = jnp.concatenate(parts, axis=0).T


def live_mask(counts):
    valid = counts[0] + counts[1] + counts[2] + counts[3]
    lane = lax.broadcasted_iota(jnp.int32, (1, 384), 1)
    i, j = lane // 128 * LOW + lane % LOW, lane % 128 // LOW
    row = lax.axis_index("x") * 4 + lax.axis_index("z_lo")
    col = lax.axis_index("y") * 4 + lax.axis_index("z_hi") * 2 + lax.axis_index("core")
    live = (row * 24 + i < valid) & (col * 12 + j < valid) & (j < 12)
    return live.astype(F32)


def column(vector, width):
    square = jnp.broadcast_to(vector.reshape(1, 128), (128, 128)).T
    return jnp.concatenate([square] * (width // 128), axis=1)


def load_tile(tile):
    x = tile[...].astype(F32)
    gap = jnp.zeros(((SLOTS - 12) * LOW, 128), F32)
    parts = []
    for i_hi in range(3):
        parts += [x[:, LOW * i_hi : LOW * (i_hi + 1)].reshape(12 * LOW, 128), gap]
    return jnp.concatenate(parts, axis=0)


def store_tile(value, scratch, tile):
    for i_hi in range(3):
        part = value[128 * i_hi : 128 * i_hi + 12 * LOW].reshape(12, LOW, 128)
        scratch[:, LOW * i_hi : LOW * (i_hi + 1), :] = part
    tile[...] = scratch[...].astype(BF16)


def third(value, i_hi):
    return value[:, 128 * i_hi : 128 * (i_hi + 1)]


def front_kernel(
    counts, pair, gain, bias, w_values, w_gates, both, values, gate, hat, inv, normed,
    rows, counts_s, pair_s, gain_s, bias_s, w_values_s, w_gates_s, sems,
):
    ends = ((pair, pair_s), (gain, gain_s), (bias, bias_s), (w_values, w_values_s), (w_gates, w_gates_s), (counts, counts_s))
    copies = [pltpu.make_async_copy(src, dst, sems.at[n]) for n, (src, dst) in enumerate(ends)]
    for copy in copies:
        copy.start()
    copies[0].wait()
    x = load_tile(pair_s)
    centre = x - jnp.mean(x, axis=1, keepdims=True)
    inv_std = lax.rsqrt(jnp.mean(centre * centre, axis=1, keepdims=True) + EPS)
    pair_hat = centre * inv_std
    for copy in copies[1:]:
        copy.wait()
    normed_b = (pair_hat * gain_s[...] + bias_s[...]).astype(BF16)
    hat[...] = pair_hat
    inv[...] = jnp.broadcast_to(inv_std, (384, 128))
    normed[...] = normed_b
    vals = dot(w_values_s[...], normed_b, (0, 1))
    sig = jax.nn.sigmoid(dot(w_gates_s[...], normed_b, (0, 1)))
    values[...] = vals
    gate[...] = sig
    out = sig * vals * live_mask(counts_s)
    for i_hi in range(3):
        rows[pl.ds(i_hi, 128, stride=6), :] = third(out[:128], i_hi)
        rows[pl.ds(3 + i_hi, 128, stride=6), :] = third(out[128:], i_hi)
    both[...] = rows[...].astype(BF16)


def gate_kernel(
    counts, normed, cotangent, values, gate, hat, inv, w_out_gate, w_out, in_gain, out_gain,
    out_sig, upstream, scaled, to_values, to_gates, hat_t, inv_t, gain_t,
):
    sig = jax.nn.sigmoid(dot(w_out_gate[...], normed[...], (0, 1)))
    up = load_tile(cotangent).T
    d_proj = (up * sig).astype(BF16)
    out_sig[...] = sig
    upstream[...] = up
    scaled[...] = dot(w_out[...], d_proj, (1, 0)) * column(out_gain[...], 384)
    live = live_mask(counts)
    sig = gate[...]
    to_values[...] = sig * live
    to_gates[...] = values[...] * sig * (1.0 - sig) * live
    hat_t[...] = hat[...].T
    inv_t[...] = inv[...].T[:8]
    gain_t[...] = column(in_gain[...], 128)


def split_kernel(both, left, right, rows, natural):
    rows[...] = both[...].astype(F32)
    matrix = to_matrix(rows, 3, 6)
    packed = []
    for t in range(3):
        natural[t] = third(matrix, t)
        packed += [jnp.concatenate([natural[t, pl.ds(slot, LOW, stride=12), :] for slot in range(12)], axis=0)]
    packed = jnp.concatenate(packed, axis=1).astype(BF16)
    for part in range(4):
        right[part] = packed
    left[...] = to_matrix(rows, 0, 6).astype(BF16)


def inner_kernel(left, right, inner, right_all, rows):
    parts = [right[part].astype(F32) for part in range(4)]
    ordered = [parts[part][LOW * slot : LOW * (slot + 1)] for slot in range(12) for part in range(4)]
    ordered = jnp.concatenate(ordered, axis=0).astype(BF16)
    right_all[...] = ordered
    to_rows(dot(left[...], ordered, (1, 1)), rows, 0, 4)
    rows[pl.ds(3, 128, stride=4), :] = jnp.zeros((128, 128), F32)
    inner[...] = rows[...].astype(BF16)


def norm_kernel(inner, scaled, d_inner, inner_hat, rows):
    rows[...] = inner[...].astype(F32)
    for i_hi in range(3):
        x = rows[pl.ds(i_hi, 128, stride=4), :]
        centre = x - jnp.mean(x, axis=0, keepdims=True)
        inv_std = lax.rsqrt(jnp.mean(centre * centre, axis=0, keepdims=True) + EPS)
        hat = centre * inv_std
        up = scaled[:, 128 * i_hi : 128 * (i_hi + 1)]
        first_mean = jnp.mean(up, axis=0, keepdims=True)
        second_mean = jnp.mean(up * hat, axis=0, keepdims=True)
        rows[pl.ds(i_hi, 128, stride=4), :] = inv_std * (up - first_mean - hat * second_mean)
        inner_hat[:, 128 * i_hi : 128 * (i_hi + 1)] = hat
    d_inner[...] = rows[...].astype(BF16)


def update_kernel(inner_hat, out_sig, upstream, out_gain, out_bias, w_out, w_out_gate, update, d_normed, tile):
    inner_n = inner_hat[...] * column(out_gain[...], 384) + column(out_bias[...], 384)
    proj = dot(w_out[...], inner_n.astype(BF16), (0, 0))
    sig = out_sig[...]
    store_tile((sig * proj).T, tile, update)
    d_gate_out = (upstream[...] * proj * sig * (1.0 - sig)).astype(BF16)
    d_normed[...] = dot(w_out_gate[...], d_gate_out, (1, 0))


def grad_kernel(d_inner, left, right_all, d_left, d_right, rows):
    rows[...] = d_inner[...].astype(F32)
    packed = to_matrix(rows, 0, 4).astype(BF16)
    sums = dot(packed, left[...], (0, 0))
    for part in range(4):
        bands = [32 * slot + LOW * part for slot in range(12)]
        d_right[part] = jnp.concatenate([sums[band : band + LOW] for band in bands], axis=0).astype(BF16)
    d_left[...] = dot(packed, right_all[...], (1, 0))


def merge_kernel(d_left, d_right, d_both, rows, natural):
    to_rows(d_left[...], rows, 0, 6)
    parts = [d_right[part].astype(F32) for part in range(4)]
    total = (parts[0] + parts[1]) + (parts[2] + parts[3])
    for t in range(3):
        for slot in range(12):
            natural[t, pl.ds(slot, LOW, stride=12), :] = third(total, t)[LOW * slot : LOW * (slot + 1)]
    to_rows(jnp.concatenate([natural[t] for t in range(3)], axis=1), rows, 3, 6)
    d_both[...] = rows[...].astype(BF16)


def back_kernel(d_both, to_values, to_gates, d_out, hat_t, inv_t, gain_t, w_values, w_gates, grad, rows, tile):
    rows[...] = d_both[...].astype(F32)
    parts = [
        jnp.concatenate([rows[pl.ds(3 * side + i_hi, 128, stride=6), :] for i_hi in range(3)], axis=1)
        for side in range(2)
    ]
    incoming = jnp.concatenate(parts, axis=0)
    d_values = (incoming * to_values[...]).astype(BF16)
    d_gates = (incoming * to_gates[...]).astype(BF16)
    d_normed = d_out[...] + dot(w_values[...], d_values, (1, 0)) + dot(w_gates[...], d_gates, (1, 0))
    scaled = d_normed * jnp.concatenate([gain_t[...]] * 3, axis=1)
    pair_hat = hat_t[...]
    first_mean = jnp.mean(scaled, axis=0, keepdims=True)
    second_mean = jnp.mean(scaled * pair_hat, axis=0, keepdims=True)
    store_tile((inv_t[:1] * (scaled - first_mean - pair_hat * second_mean)).T, tile, grad)


def call(kernel, outs, args, scratch=(), scalars=0, flops=0, last=0):
    vmem, smem = pl.BlockSpec(memory_space=pltpu.VMEM), pl.BlockSpec(memory_space=pltpu.SMEM)
    size = sum(a.size * a.dtype.itemsize for a in args)
    shapes = [jax.ShapeDtypeStruct(*out) if n < last else pltpu.VMEM(*out) for n, out in enumerate(outs)]
    return pl.pallas_call(
        kernel,
        out_shape=shapes,
        in_specs=[smem] * scalars + [vmem] * (len(args) - scalars),
        out_specs=[vmem] * len(outs),
        scratch_shapes=[pltpu.VMEM(shape, F32) for shape in scratch],
        compiler_params=pltpu.CompilerParams(vmem_limit_bytes=24 * 1024 * 1024),
        cost_estimate=pl.CostEstimate(flops=flops, bytes_accessed=size, transcendentals=0),
    )(*args)


def call_front(outs, args, rows):
    args = [pltpu.with_memory_space_constraint(arg, pltpu.HBM) for arg in args]
    spaces = [pltpu.SMEM] + [pltpu.VMEM] * 5
    held = [space(arg.shape, arg.dtype) for space, arg in zip(spaces, args)]
    return pl.pallas_call(
        front_kernel,
        out_shape=[pltpu.VMEM(*out) for out in outs],
        in_specs=[pl.BlockSpec(memory_space=pltpu.HBM)] * 6,
        out_specs=[pl.BlockSpec(memory_space=pltpu.VMEM)] * len(outs),
        scratch_shapes=[pltpu.VMEM(rows, F32)] + held + [pltpu.SemaphoreType.DMA((6,))],
        compiler_params=pltpu.CompilerParams(vmem_limit_bytes=24 * 1024 * 1024),
    )(*args)


def exchange(rows):
    return lax.all_to_all(rows.reshape(128, -1, 2, 128), GROUP, 0, 0).reshape(rows.shape)


def shards(
    pair,
    cotangent,
    chain_counts,
    in_gain,
    in_bias,
    w_values,
    w_gates,
    w_out_gate,
    out_gain,
    out_bias,
    w_out,
):
    pair, cotangent = pair.transpose(1, 0, 2), cotangent.transpose(1, 0, 2)
    wide, tall, tokens, tile = (256, 384), (128, 384), (384, 128), (12, 24, 128)
    one, two = (512, 128), (768, 128)
    both, values, gate, hat, inv, normed = call_front(
        [(two, BF16), (wide, F32), (wide, F32), (tokens, F32), (tokens, F32), (tokens, BF16)],
        [chain_counts, pair, in_gain.reshape(1, 128), in_bias.reshape(1, 128), w_values, w_gates],
        two,
    )
    both = exchange(both)
    out_sig, upstream, scaled, to_values, to_gates, hat_t, inv_t, gain_t = call(
        gate_kernel,
        [(tall, F32)] * 3 + [(wide, F32)] * 2 + [(tall, F32), ((8, 384), F32), ((128, 128), F32)],
        [chain_counts, normed, cotangent, values, gate, hat, inv, w_out_gate, w_out, in_gain, out_gain],
        scalars=1,
    )
    left, right = call(split_kernel, [((96, 384), BF16), ((4, 96, 384), BF16)], [both], [two, (3, 96, 128)])
    right = lax.all_to_all(right, "x", 0, 0)
    inner, right = call(inner_kernel, [(one, BF16), ((384, 384), BF16)], [left, right], [one])
    inner = exchange(inner)
    d_inner, inner_hat = call(norm_kernel, [(one, BF16), (tall, F32)], [inner, scaled], [one])
    d_inner = exchange(d_inner)
    update, d_out = call(
        update_kernel,
        [(tile, BF16), (tall, F32)],
        [inner_hat, out_sig, upstream, out_gain, out_bias, w_out, w_out_gate],
        [tile],
        last=1,
    )
    d_left, d_right = call(
        grad_kernel, [((96, 384), F32), ((4, 96, 384), BF16)], [d_inner, left, right], [one]
    )
    d_right = lax.all_to_all(d_right, "x", 0, 0)
    (d_both,) = call(merge_kernel, [(two, BF16)], [d_left, d_right], [two, (3, 96, 128)])
    d_both = exchange(d_both)
    (grad,) = call(
        back_kernel,
        [(tile, BF16)],
        [d_both, to_values, to_gates, d_out, hat_t, inv_t, gain_t, w_values, w_gates],
        [two, tile],
        last=1,
    )
    return (update.transpose(1, 0, 2), grad.transpose(1, 0, 2))


def solution(mesh):
    fine = Mesh(mesh.devices.reshape(4, 4, 8, 2, 2), ROW + COL)
    placed = P(ROW, COL, None)
    return jax.shard_map(
        shards,
        mesh=fine,
        in_specs=(placed, placed) + (P(),) * 9,
        out_specs=(placed, placed),
        check_vma=False,
    )
```

```python
import jax
import jax.numpy as jnp
from jax import lax
from jax.experimental import pallas as pl
from jax.experimental.pallas import tpu as pltpu
from jax.sharding import Mesh
from jax.sharding import PartitionSpec as P

EPS = 1e-05
F32 = jnp.float32
BF16 = jnp.bfloat16
ROW = ("x", "z_lo")
COL = ("y", "z_hi", "core")
GROUP = ("z_lo",) + COL
SLOTS = 16
LOW = 8


def dot(a, b, contract):
    return lax.dot_general(a, b, ((contract[:1], contract[1:]), ((), ())), preferred_element_type=F32)


def swap_quads(quad):
    lane = lax.broadcasted_iota(jnp.int32, (LOW, 128), 1)
    quad = list(quad)
    for step in (2, 1):
        low = (lane & (32 * step)) == 0
        for a in range(4):
            if a & step == 0:
                one, two = quad[a], quad[a + step]
                quad[a] = jnp.where(low, one, pltpu.roll(two, 32 * step, 1))
                quad[a + step] = jnp.where(low, pltpu.roll(one, 128 - 32 * step, 1), two)
    return quad


def to_matrix(rows, first, per):
    bands = {}
    for i_hi in range(3):
        turned = rows[pl.ds(first + i_hi, 128, stride=per), :].T
        for j_hi in range(3):
            parts = [turned[LOW * (4 * j_hi + j_lo) : LOW * (4 * j_hi + j_lo + 1)] for j_lo in range(4)]
            for z, part in enumerate(swap_quads(parts)):
                bands[z, i_hi, j_hi] = part
    return jnp.concatenate(
        [
            jnp.concatenate([bands[z, i_hi, j_hi] for j_hi in range(3)], axis=1)
            for z in range(4)
            for i_hi in range(3)
        ],
        axis=0,
    )


def to_rows(matrix, rows, first, per):
    for i_hi in range(3):
        parts = []
        for j_hi in range(3):
            bands = [24 * z + LOW * i_hi for z in range(4)]
            parts += swap_quads([matrix[band : band + LOW, 128 * j_hi : 128 * (j_hi + 1)] for band in bands])
        parts += [jnp.zeros(((SLOTS - 12) * LOW, 128), F32)]
        rows[pl.ds(first + i_hi, 128, stride=per), :] = jnp.concatenate(parts, axis=0).T


def live_mask(counts):
    valid = counts[0] + counts[1] + counts[2] + counts[3]
    lane = lax.broadcasted_iota(jnp.int32, (1, 384), 1)
    i, j = lane // 128 * LOW + lane % LOW, lane % 128 // LOW
    row = lax.axis_index("x") * 4 + lax.axis_index("z_lo")
    col = lax.axis_index("y") * 4 + lax.axis_index("z_hi") * 2 + lax.axis_index("core")
    live = (row * 24 + i < valid) & (col * 12 + j < valid) & (j < 12)
    return live.astype(F32)


def columns(*vectors):
    spare = jnp.zeros((128 - len(vectors), 128), F32)
    return jnp.concatenate([*vectors, spare], axis=0).T


def load_tile(tile):
    x = tile[...].astype(F32)
    gap = jnp.zeros(((SLOTS - 12) * LOW, 128), F32)
    parts = []
    for i_hi in range(3):
        parts += [x[:, LOW * i_hi : LOW * (i_hi + 1)].reshape(12 * LOW, 128), gap]
    return jnp.concatenate(parts, axis=0)


def store_tile(value, scratch, tile):
    for i_hi in range(3):
        part = value[128 * i_hi : 128 * i_hi + 12 * LOW].reshape(12, LOW, 128)
        scratch[:, LOW * i_hi : LOW * (i_hi + 1), :] = part
    tile[...] = scratch[...].astype(BF16)


def third(value, i_hi):
    return value[:, 128 * i_hi : 128 * (i_hi + 1)]


def front_kernel(*refs):
    ends, (both, scaled, out_sig, upstream, to_values, to_gates, hat, inv, cols) = refs[:11], refs[11:20]
    rows, held, sems = refs[20], refs[21:32], refs[32]
    copies = [pltpu.make_async_copy(src, dst, sems.at[n]) for n, (src, dst) in enumerate(zip(ends, held))]
    for copy in copies:
        copy.start()
    pair, cotangent, in_gain, in_bias, out_gain, out_bias, w_values, w_gates, w_out_gate, w_out, counts = held
    copies[0].wait()
    x = load_tile(pair).T
    centre = x - jnp.mean(x, axis=0, keepdims=True)
    inv_std = lax.rsqrt(jnp.mean(centre * centre, axis=0, keepdims=True) + EPS)
    pair_hat = centre * inv_std
    hat[...] = pair_hat
    inv[...] = jnp.broadcast_to(inv_std, (8, 384))
    for copy in copies[1:]:
        copy.wait()
    vectors = columns(in_gain[...], in_bias[...], out_gain[...], out_bias[...])
    cols[...] = vectors
    normed_b = (pair_hat * vectors[:, 0:1] + vectors[:, 1:2]).astype(BF16)
    vals = dot(w_values[...], normed_b, (0, 0))
    sig = jax.nn.sigmoid(dot(w_gates[...], normed_b, (0, 0)))
    live = live_mask(counts)
    sig_live = sig * live
    out = sig_live * vals
    for i_hi in range(3):
        rows[pl.ds(i_hi, 128, stride=6), :] = third(out[:128], i_hi)
        rows[pl.ds(3 + i_hi, 128, stride=6), :] = third(out[128:], i_hi)
    both[...] = rows[...].astype(BF16)
    to_values[...] = sig_live
    to_gates[...] = out * (1.0 - sig)
    sig = jax.nn.sigmoid(dot(w_out_gate[...], normed_b, (0, 0)))
    up = load_tile(cotangent).T
    out_sig[...] = sig
    upstream[...] = up
    scaled[...] = dot(w_out[...], (up * sig).astype(BF16), (1, 0)) * vectors[:, 2:3]


def split_kernel(both, left, right, rows, natural):
    rows[...] = both[...].astype(F32)
    matrix = to_matrix(rows, 3, 6)
    packed = []
    for t in range(3):
        natural[t] = third(matrix, t)
        packed += [jnp.concatenate([natural[t, pl.ds(slot, LOW, stride=12), :] for slot in range(12)], axis=0)]
    packed = jnp.concatenate(packed, axis=1).astype(BF16)
    for part in range(4):
        right[part] = packed
    left[...] = to_matrix(rows, 0, 6).astype(BF16)


def inner_kernel(left, right, inner, right_all, rows):
    parts = [right[part].astype(F32) for part in range(4)]
    ordered = [parts[part][LOW * slot : LOW * (slot + 1)] for slot in range(12) for part in range(4)]
    ordered = jnp.concatenate(ordered, axis=0).astype(BF16)
    right_all[...] = ordered
    to_rows(dot(left[...], ordered, (1, 1)), rows, 0, 4)
    rows[pl.ds(3, 128, stride=4), :] = jnp.zeros((128, 128), F32)
    inner[...] = rows[...].astype(BF16)


def norm_kernel(inner, scaled, d_inner, inner_hat, rows):
    rows[...] = inner[...].astype(F32)
    for i_hi in range(3):
        x = rows[pl.ds(i_hi, 128, stride=4), :]
        centre = x - jnp.mean(x, axis=0, keepdims=True)
        inv_std = lax.rsqrt(jnp.mean(centre * centre, axis=0, keepdims=True) + EPS)
        hat = centre * inv_std
        up = scaled[:, 128 * i_hi : 128 * (i_hi + 1)]
        first_mean = jnp.mean(up, axis=0, keepdims=True)
        second_mean = jnp.mean(up * hat, axis=0, keepdims=True)
        rows[pl.ds(i_hi, 128, stride=4), :] = inv_std * (up - first_mean - hat * second_mean)
        inner_hat[:, 128 * i_hi : 128 * (i_hi + 1)] = hat
    d_inner[...] = rows[...].astype(BF16)


def grad_kernel(d_inner, left, right_all, d_left, d_right, rows):
    rows[...] = d_inner[...].astype(F32)
    packed = to_matrix(rows, 0, 4).astype(BF16)
    sums = dot(packed, left[...], (0, 0))
    for part in range(4):
        bands = [32 * slot + LOW * part for slot in range(12)]
        d_right[part] = jnp.concatenate([sums[band : band + LOW] for band in bands], axis=0).astype(BF16)
    d_left[...] = dot(packed, right_all[...], (1, 0))


def merge_kernel(d_left, d_right, d_both, rows, natural):
    to_rows(d_left[...], rows, 0, 6)
    parts = [d_right[part].astype(F32) for part in range(4)]
    total = (parts[0] + parts[1]) + (parts[2] + parts[3])
    for t in range(3):
        for slot in range(12):
            natural[t, pl.ds(slot, LOW, stride=12), :] = third(total, t)[LOW * slot : LOW * (slot + 1)]
    to_rows(jnp.concatenate([natural[t] for t in range(3)], axis=1), rows, 3, 6)
    d_both[...] = rows[...].astype(BF16)


def back_kernel(
    d_both, to_values, to_gates, hat, inv, cols, inner_hat, out_sig, upstream,
    w_values, w_gates, w_out_gate, w_out, update, grad, rows, tile,
):
    vectors = cols[...]
    inner_n = inner_hat[...] * vectors[:, 2:3] + vectors[:, 3:4]
    proj = dot(w_out[...], inner_n.astype(BF16), (0, 0))
    sig = out_sig[...]
    gated = sig * proj
    store_tile(gated.T, tile, update)
    d_gate_out = (upstream[...] * gated * (1.0 - sig)).astype(BF16)
    rows[...] = d_both[...].astype(F32)
    parts = [
        jnp.concatenate([rows[pl.ds(3 * side + i_hi, 128, stride=6), :] for i_hi in range(3)], axis=1)
        for side in range(2)
    ]
    incoming = jnp.concatenate(parts, axis=0)
    d_values = (incoming * to_values[...]).astype(BF16)
    d_gates = (incoming * to_gates[...]).astype(BF16)
    d_normed = dot(w_out_gate[...], d_gate_out, (1, 0))
    d_normed += dot(w_values[...], d_values, (1, 0)) + dot(w_gates[...], d_gates, (1, 0))
    up = d_normed * vectors[:, 0:1]
    pair_hat = hat[...]
    first_mean = jnp.mean(up, axis=0, keepdims=True)
    second_mean = jnp.mean(up * pair_hat, axis=0, keepdims=True)
    store_tile((inv[:1] * (up - first_mean - pair_hat * second_mean)).T, tile, grad)


def call(kernel, outs, args, scratch=(), last=False):
    vmem = pl.BlockSpec(memory_space=pltpu.VMEM)
    space = jax.ShapeDtypeStruct if last else pltpu.VMEM
    return pl.pallas_call(
        kernel,
        out_shape=[space(*out) for out in outs],
        in_specs=[vmem] * len(args),
        out_specs=[vmem] * len(outs),
        scratch_shapes=[pltpu.VMEM(shape, F32) for shape in scratch],
        compiler_params=pltpu.CompilerParams(vmem_limit_bytes=24 * 1024 * 1024),
    )(*args)


def call_front(outs, args, rows):
    args = [pltpu.with_memory_space_constraint(arg, pltpu.HBM) for arg in args]
    spaces = [pltpu.VMEM] * (len(args) - 1) + [pltpu.SMEM]
    held = [space(arg.shape, arg.dtype) for space, arg in zip(spaces, args)]
    return pl.pallas_call(
        front_kernel,
        out_shape=[pltpu.VMEM(*out) for out in outs],
        in_specs=[pl.BlockSpec(memory_space=pltpu.HBM)] * len(args),
        out_specs=[pl.BlockSpec(memory_space=pltpu.VMEM)] * len(outs),
        scratch_shapes=[pltpu.VMEM(rows, F32)] + held + [pltpu.SemaphoreType.DMA((len(args),))],
        compiler_params=pltpu.CompilerParams(vmem_limit_bytes=24 * 1024 * 1024),
    )(*args)


def exchange(rows):
    return lax.all_to_all(rows.reshape(128, -1, 2, 128), GROUP, 0, 0).reshape(rows.shape)


def shards(
    pair,
    cotangent,
    chain_counts,
    in_gain,
    in_bias,
    w_values,
    w_gates,
    w_out_gate,
    out_gain,
    out_bias,
    w_out,
):
    pair, cotangent = pair.transpose(1, 0, 2), cotangent.transpose(1, 0, 2)
    wide, tall, tile = (256, 384), (128, 384), (12, 24, 128)
    one, two = (512, 128), (768, 128)
    vectors = [vector.reshape(1, 128) for vector in (in_gain, in_bias, out_gain, out_bias)]
    both, scaled, out_sig, upstream, to_values, to_gates, hat, inv, cols = call_front(
        [(two, BF16)]
        + [(tall, F32)] * 3
        + [(wide, F32)] * 2
        + [(tall, F32), ((8, 384), F32), ((128, 128), F32)],
        [pair, cotangent, *vectors, w_values, w_gates, w_out_gate, w_out, chain_counts],
        two,
    )
    both = exchange(both)
    left, right = call(
        split_kernel, [((96, 384), BF16), ((4, 96, 384), BF16)], [both], [two, (3, 96, 128)]
    )
    right = lax.all_to_all(right, "x", 0, 0)
    inner, right = call(inner_kernel, [(one, BF16), ((384, 384), BF16)], [left, right], [one])
    inner = exchange(inner)
    d_inner, inner_hat = call(norm_kernel, [(one, BF16), (tall, F32)], [inner, scaled], [one])
    d_inner = exchange(d_inner)
    d_left, d_right = call(
        grad_kernel, [((96, 384), F32), ((4, 96, 384), BF16)], [d_inner, left, right], [one]
    )
    d_right = lax.all_to_all(d_right, "x", 0, 0)
    (d_both,) = call(merge_kernel, [(two, BF16)], [d_left, d_right], [two, (3, 96, 128)])
    d_both = exchange(d_both)
    update, grad = call(
        back_kernel,
        [(tile, BF16)] * 2,
        [
            d_both, to_values, to_gates, hat, inv, cols, inner_hat, out_sig, upstream,
            w_values, w_gates, w_out_gate, w_out,
        ],
        [two, tile],
        last=True,
    )
    return (update.transpose(1, 0, 2), grad.transpose(1, 0, 2))


def solution(mesh):
    fine = Mesh(mesh.devices.reshape(4, 4, 8, 2, 2), ROW + COL)
    placed = P(ROW, COL, None)
    return jax.shard_map(
        shards,
        mesh=fine,
        in_specs=(placed, placed) + (P(),) * 9,
        out_specs=(placed, placed),
        check_vma=False,
    )
```

```python
import jax
import jax.numpy as jnp
from jax import lax
from jax.experimental import pallas as pl
from jax.experimental.pallas import tpu as pltpu
from jax.sharding import Mesh
from jax.sharding import PartitionSpec as P

EPS = 1e-05
F32 = jnp.float32
BF16 = jnp.bfloat16
ROW = ("x", "z_lo")
COL = ("y", "z_hi", "core")
GROUP = ("z_lo",) + COL
SLOTS = 16
LOW = 8


def dot(a, b, contract):
    return lax.dot_general(a, b, ((contract[:1], contract[1:]), ((), ())), preferred_element_type=F32)


def swap_quads(quad):
    lane = lax.broadcasted_iota(jnp.int32, (LOW, 128), 1)
    quad = list(quad)
    for step in (2, 1):
        low = (lane & (32 * step)) == 0
        for a in range(4):
            if a & step == 0:
                one, two = quad[a], quad[a + step]
                quad[a] = jnp.where(low, one, pltpu.roll(two, 32 * step, 1))
                quad[a + step] = jnp.where(low, pltpu.roll(one, 128 - 32 * step, 1), two)
    return quad


def to_matrix(rows, first, per):
    bands = {}
    for i_hi in range(3):
        turned = rows[pl.ds(first + i_hi, 128, stride=per), :].T
        for j_hi in range(3):
            parts = [turned[LOW * (4 * j_hi + j_lo) : LOW * (4 * j_hi + j_lo + 1)] for j_lo in range(4)]
            for z, part in enumerate(swap_quads(parts)):
                bands[z, i_hi, j_hi] = part
    return jnp.concatenate(
        [
            jnp.concatenate([bands[z, i_hi, j_hi] for j_hi in range(3)], axis=1)
            for z in range(4)
            for i_hi in range(3)
        ],
        axis=0,
    )


def to_rows(matrix, rows, first, per):
    for i_hi in range(3):
        parts = []
        for j_hi in range(3):
            bands = [24 * z + LOW * i_hi for z in range(4)]
            parts += swap_quads([matrix[band : band + LOW, 128 * j_hi : 128 * (j_hi + 1)] for band in bands])
        parts += [jnp.zeros(((SLOTS - 12) * LOW, 128), F32)]
        rows[pl.ds(first + i_hi, 128, stride=per), :] = jnp.concatenate(parts, axis=0).T


def live_mask(counts):
    valid = counts[0] + counts[1] + counts[2] + counts[3]
    lane = lax.broadcasted_iota(jnp.int32, (1, 384), 1)
    i, j = lane // 128 * LOW + lane % LOW, lane % 128 // LOW
    row = lax.axis_index("x") * 4 + lax.axis_index("z_lo")
    col = lax.axis_index("y") * 4 + lax.axis_index("z_hi") * 2 + lax.axis_index("core")
    live = (row * 24 + i < valid) & (col * 12 + j < valid) & (j < 12)
    return live.astype(F32)


def columns(*vectors):
    spare = jnp.zeros((128 - len(vectors), 128), F32)
    return jnp.concatenate([*vectors, spare], axis=0).T


def load_tile(tile):
    x = tile[...].astype(F32)
    gap = jnp.zeros(((SLOTS - 12) * LOW, 128), F32)
    parts = []
    for i_hi in range(3):
        parts += [x[:, LOW * i_hi : LOW * (i_hi + 1)].reshape(12 * LOW, 128), gap]
    return jnp.concatenate(parts, axis=0)


def store_tile(value, scratch, tile):
    for i_hi in range(3):
        part = value[128 * i_hi : 128 * i_hi + 12 * LOW].reshape(12, LOW, 128)
        scratch[:, LOW * i_hi : LOW * (i_hi + 1), :] = part
    tile[...] = scratch[...].astype(BF16)


def third(value, i_hi):
    return value[:, 128 * i_hi : 128 * (i_hi + 1)]


def front_kernel(*refs):
    ends, (both, scaled, out_sig, upstream, to_values, to_gates, hat, inv, cols) = refs[:11], refs[11:20]
    rows, held, sems = refs[20], refs[21:32], refs[32]
    copies = [pltpu.make_async_copy(src, dst, sems.at[n]) for n, (src, dst) in enumerate(zip(ends, held))]
    for copy in copies:
        copy.start()
    pair, cotangent, in_gain, in_bias, out_gain, out_bias, w_values, w_gates, w_out_gate, w_out, counts = held
    for copy in copies:
        copy.wait()
    vectors = columns(in_gain[...], in_bias[...], out_gain[...], out_bias[...])
    cols[...] = vectors
    live_all = live_mask(counts)
    tile_x, tile_up = load_tile(pair), load_tile(cotangent)
    for i_hi in range(3):
        lanes = slice(128 * i_hi, 128 * (i_hi + 1))
        x = tile_x[lanes].T
        centre = x - jnp.mean(x, axis=0, keepdims=True)
        inv_std = lax.rsqrt(jnp.mean(centre * centre, axis=0, keepdims=True) + EPS)
        pair_hat = centre * inv_std
        hat[:, lanes] = pair_hat
        inv[:, lanes] = jnp.broadcast_to(inv_std, (8, 128))
        normed_b = (pair_hat * vectors[:, 0:1] + vectors[:, 1:2]).astype(BF16)
        vals = dot(w_values[...], normed_b, (0, 0))
        sig = jax.nn.sigmoid(dot(w_gates[...], normed_b, (0, 0)))
        sig_live = sig * third(live_all, i_hi)
        out = sig_live * vals
        rows[pl.ds(i_hi, 128, stride=6), :] = out[:128]
        rows[pl.ds(3 + i_hi, 128, stride=6), :] = out[128:]
        to_values[:, lanes] = sig_live
        to_gates[:, lanes] = out * (1.0 - sig)
        sig = jax.nn.sigmoid(dot(w_out_gate[...], normed_b, (0, 0)))
        up = tile_up[lanes].T
        out_sig[:, lanes] = sig
        upstream[:, lanes] = up.astype(BF16)
        scaled[:, lanes] = dot(w_out[...], (up * sig).astype(BF16), (1, 0)) * vectors[:, 2:3]
    both[...] = rows[:768].astype(BF16)


def split_kernel(both, left, right, rows, natural):
    rows[:768] = both[...].astype(F32)
    matrix = to_matrix(rows, 3, 6)
    packed = []
    for t in range(3):
        natural[t, :96] = third(matrix, t)
        packed += [jnp.concatenate([natural[t, pl.ds(slot, LOW, stride=12), :] for slot in range(12)], axis=0)]
    packed = jnp.concatenate(packed, axis=1).astype(BF16)
    for part in range(4):
        right[part] = packed
    left[...] = to_matrix(rows, 0, 6).astype(BF16)


def inner_kernel(left, right, inner, right_all, rows):
    parts = [right[part].astype(F32) for part in range(4)]
    ordered = [parts[part][LOW * slot : LOW * (slot + 1)] for slot in range(12) for part in range(4)]
    ordered = jnp.concatenate(ordered, axis=0).astype(BF16)
    right_all[...] = ordered
    to_rows(dot(left[...], ordered, (1, 1)), rows, 0, 4)
    rows[pl.ds(3, 128, stride=4), :] = jnp.zeros((128, 128), F32)
    inner[...] = rows[:512].astype(BF16)


def norm_kernel(inner, scaled, d_inner, inner_hat, rows):
    rows[:512] = inner[...].astype(F32)
    for i_hi in range(3):
        x = rows[pl.ds(i_hi, 128, stride=4), :]
        centre = x - jnp.mean(x, axis=0, keepdims=True)
        inv_std = lax.rsqrt(jnp.mean(centre * centre, axis=0, keepdims=True) + EPS)
        hat = centre * inv_std
        up = scaled[:, 128 * i_hi : 128 * (i_hi + 1)]
        first_mean = jnp.mean(up, axis=0, keepdims=True)
        second_mean = jnp.mean(up * hat, axis=0, keepdims=True)
        rows[pl.ds(i_hi, 128, stride=4), :] = inv_std * (up - first_mean - hat * second_mean)
        inner_hat[:, 128 * i_hi : 128 * (i_hi + 1)] = hat
    d_inner[...] = rows[:512].astype(BF16)


def grad_kernel(d_inner, left, right_all, d_left, d_right, rows):
    rows[:512] = d_inner[...].astype(F32)
    packed = to_matrix(rows, 0, 4).astype(BF16)
    sums = dot(packed, left[...], (0, 0))
    for part in range(4):
        bands = [32 * slot + LOW * part for slot in range(12)]
        d_right[part] = jnp.concatenate([sums[band : band + LOW] for band in bands], axis=0).astype(BF16)
    d_left[...] = dot(packed, right_all[...], (1, 0))


def merge_kernel(d_left, d_right, d_both, rows, natural):
    to_rows(d_left[...], rows, 0, 6)
    parts = [d_right[part].astype(F32) for part in range(4)]
    total = (parts[0] + parts[1]) + (parts[2] + parts[3])
    for t in range(3):
        for slot in range(12):
            natural[t, pl.ds(slot, LOW, stride=12), :] = third(total, t)[LOW * slot : LOW * (slot + 1)]
    to_rows(jnp.concatenate([natural[t, :96] for t in range(3)], axis=1), rows, 3, 6)
    d_both[...] = rows[:768].astype(BF16)


def back_kernel(
    d_both, to_values, to_gates, hat, inv, cols, inner_hat, out_sig, upstream,
    w_values, w_gates, w_out_gate, w_out, update, grad, rows, tile,
):
    vectors = cols[...]
    inner_n = inner_hat[...] * vectors[:, 2:3] + vectors[:, 3:4]
    proj = dot(w_out[...], inner_n.astype(BF16), (0, 0))
    sig = out_sig[...]
    gated = sig * proj
    store_tile(gated.T, tile, update)
    d_gate_out = (upstream[...].astype(F32) * gated * (1.0 - sig)).astype(BF16)
    rows[:768] = d_both[...].astype(F32)
    parts = [
        jnp.concatenate([rows[pl.ds(3 * side + i_hi, 128, stride=6), :] for i_hi in range(3)], axis=1)
        for side in range(2)
    ]
    incoming = jnp.concatenate(parts, axis=0)
    d_values = (incoming * to_values[...]).astype(BF16)
    d_gates = (incoming * to_gates[...]).astype(BF16)
    d_normed = dot(w_out_gate[...], d_gate_out, (1, 0))
    d_normed += dot(w_values[...], d_values, (1, 0)) + dot(w_gates[...], d_gates, (1, 0))
    up = d_normed * vectors[:, 0:1]
    pair_hat = hat[...]
    first_mean = jnp.mean(up, axis=0, keepdims=True)
    second_mean = jnp.mean(up * pair_hat, axis=0, keepdims=True)
    store_tile((inv[:1] * (up - first_mean - pair_hat * second_mean)).T, tile, grad)


def call(kernel, outs, args, scratch=(), last=False):
    vmem = pl.BlockSpec(memory_space=pltpu.VMEM)
    space = jax.ShapeDtypeStruct if last else pltpu.VMEM
    return pl.pallas_call(
        kernel,
        out_shape=[space(*out) for out in outs],
        in_specs=[vmem] * len(args),
        out_specs=[vmem] * len(outs),
        scratch_shapes=[pltpu.VMEM(shape, F32) for shape in scratch],
        compiler_params=pltpu.CompilerParams(vmem_limit_bytes=24 * 1024 * 1024),
    )(*args)


def call_front(outs, args, rows):
    args = [pltpu.with_memory_space_constraint(arg, pltpu.HBM) for arg in args]
    spaces = [pltpu.VMEM] * (len(args) - 1) + [pltpu.SMEM]
    held = [space(arg.shape, arg.dtype) for space, arg in zip(spaces, args)]
    return pl.pallas_call(
        front_kernel,
        out_shape=[pltpu.VMEM(*out) for out in outs],
        in_specs=[pl.BlockSpec(memory_space=pltpu.HBM)] * len(args),
        out_specs=[pl.BlockSpec(memory_space=pltpu.VMEM)] * len(outs),
        scratch_shapes=[pltpu.VMEM(rows, F32)] + held + [pltpu.SemaphoreType.DMA((len(args),))],
        compiler_params=pltpu.CompilerParams(vmem_limit_bytes=24 * 1024 * 1024),
    )(*args)


def exchange(rows):
    return lax.all_to_all(rows.reshape(128, -1, 2, 128), GROUP, 0, 0).reshape(rows.shape)


def shards(
    pair,
    cotangent,
    chain_counts,
    in_gain,
    in_bias,
    w_values,
    w_gates,
    w_out_gate,
    out_gain,
    out_bias,
    w_out,
):
    pair, cotangent = pair.transpose(1, 0, 2), cotangent.transpose(1, 0, 2)
    wide, tall, tile = (256, 384), (128, 384), (12, 24, 128)
    one, two = (512, 128), (768, 128)
    one_rows, two_rows, natural = (520, 128), (776, 128), (3, 112, 128)
    vectors = [vector.reshape(1, 128) for vector in (in_gain, in_bias, out_gain, out_bias)]
    both, scaled, out_sig, upstream, to_values, to_gates, hat, inv, cols = call_front(
        [(two, BF16)]
        + [(tall, F32)] * 2
        + [(tall, BF16)]
        + [(wide, F32)] * 2
        + [(tall, F32), ((8, 384), F32), ((128, 128), F32)],
        [pair, cotangent, *vectors, w_values, w_gates, w_out_gate, w_out, chain_counts],
        two_rows,
    )
    both = exchange(both)
    left, right = call(
        split_kernel, [((96, 384), BF16), ((4, 96, 384), BF16)], [both], [two_rows, natural]
    )
    right = lax.all_to_all(right, "x", 0, 0)
    inner, right = call(inner_kernel, [(one, BF16), ((384, 384), BF16)], [left, right], [one_rows])
    inner = exchange(inner)
    d_inner, inner_hat = call(norm_kernel, [(one, BF16), (tall, F32)], [inner, scaled], [one_rows])
    d_inner = exchange(d_inner)
    d_left, d_right = call(
        grad_kernel, [((96, 384), F32), ((4, 96, 384), BF16)], [d_inner, left, right], [one_rows]
    )
    d_right = lax.all_to_all(d_right, "x", 0, 0)
    (d_both,) = call(merge_kernel, [(two, BF16)], [d_left, d_right], [two_rows, natural])
    d_both = exchange(d_both)
    update, grad = call(
        back_kernel,
        [(tile, BF16)] * 2,
        [
            d_both, to_values, to_gates, hat, inv, cols, inner_hat, out_sig, upstream,
            w_values, w_gates, w_out_gate, w_out,
        ],
        [two_rows, tile],
        last=True,
    )
    return (update.transpose(1, 0, 2), grad.transpose(1, 0, 2))


def solution(mesh):
    fine = Mesh(mesh.devices.reshape(4, 4, 8, 2, 2), ROW + COL)
    placed = P(ROW, COL, None)
    return jax.shard_map(
        shards,
        mesh=fine,
        in_specs=(placed, placed) + (P(),) * 9,
        out_specs=(placed, placed),
        check_vma=False,
    )
```

```python
import jax
import jax.numpy as jnp
from jax import lax
from jax.experimental import pallas as pl
from jax.experimental.pallas import tpu as pltpu
from jax.sharding import Mesh
from jax.sharding import PartitionSpec as P

EPS = 1e-05
F32 = jnp.float32
BF16 = jnp.bfloat16
ROW = ("x", "z_lo")
COL = ("y", "z_hi", "core")
GROUP = ("z_lo",) + COL
SLOTS = 16
LOW = 8


def dot(a, b, contract):
    return lax.dot_general(a, b, ((contract[:1], contract[1:]), ((), ())), preferred_element_type=F32)


def swap_quads(quad):
    return [jnp.concatenate([part[:, 32 * b : 32 * (b + 1)] for part in quad], axis=1) for b in range(4)]


def to_matrix(rows, first, per):
    bands = {}
    for i_hi in range(3):
        turned = rows[pl.ds(first + i_hi, 128, stride=per), :].T
        for j_hi in range(3):
            parts = [turned[LOW * (4 * j_hi + j_lo) : LOW * (4 * j_hi + j_lo + 1)] for j_lo in range(4)]
            for z, part in enumerate(swap_quads(parts)):
                bands[z, i_hi, j_hi] = part
    return jnp.concatenate(
        [
            jnp.concatenate([bands[z, i_hi, j_hi] for j_hi in range(3)], axis=1)
            for z in range(4)
            for i_hi in range(3)
        ],
        axis=0,
    )


def to_rows(matrix, rows, first, per):
    pieces = [(i_hi, j_hi) for i_hi in range(3) for j_hi in range(3)]
    quad = []
    for z in range(4):
        bands = [
            matrix[24 * z + LOW * i_hi : 24 * z + LOW * (i_hi + 1), 128 * j_hi : 128 * (j_hi + 1)]
            for i_hi, j_hi in pieces
        ]
        quad += [jnp.concatenate(bands, axis=0)]
    quad = swap_quads(quad)
    for i_hi in range(3):
        parts = [part[LOW * n : LOW * (n + 1)] for n in range(3 * i_hi, 3 * i_hi + 3) for part in quad]
        parts += [jnp.zeros(((SLOTS - 12) * LOW, 128), F32)]
        rows[pl.ds(first + i_hi, 128, stride=per), :] = jnp.concatenate(parts, axis=0).T


def live_mask(counts):
    valid = counts[0] + counts[1] + counts[2] + counts[3]
    lane = lax.broadcasted_iota(jnp.int32, (1, 384), 1)
    i, j = lane // 128 * LOW + lane % LOW, lane % 128 // LOW
    row = lax.axis_index("x") * 4 + lax.axis_index("z_lo")
    col = lax.axis_index("y") * 4 + lax.axis_index("z_hi") * 2 + lax.axis_index("core")
    live = (row * 24 + i < valid) & (col * 12 + j < valid) & (j < 12)
    return live.astype(F32)


def columns(*vectors):
    spare = jnp.zeros((128 - len(vectors), 128), F32)
    return jnp.concatenate([*vectors, spare], axis=0).T


def load_tile(tile):
    x = tile[...].astype(F32)
    gap = jnp.zeros(((SLOTS - 12) * LOW, 128), F32)
    parts = []
    for i_hi in range(3):
        parts += [x[:, LOW * i_hi : LOW * (i_hi + 1)].reshape(12 * LOW, 128), gap]
    return jnp.concatenate(parts, axis=0)


def store_tile(value, scratch, tile):
    for i_hi in range(3):
        part = value[128 * i_hi : 128 * i_hi + 12 * LOW].reshape(12, LOW, 128)
        scratch[:, LOW * i_hi : LOW * (i_hi + 1), :] = part
    tile[...] = scratch[...].astype(BF16)


def third(value, i_hi):
    return value[:, 128 * i_hi : 128 * (i_hi + 1)]


def front_kernel(*refs):
    ends, (both, scaled, out_sig, upstream, to_values, to_gates, hat, inv, cols) = refs[:11], refs[11:20]
    rows, held, sems = refs[20], refs[21:32], refs[32]
    copies = [pltpu.make_async_copy(src, dst, sems.at[n]) for n, (src, dst) in enumerate(zip(ends, held))]
    for copy in copies:
        copy.start()
    pair, cotangent, in_gain, in_bias, out_gain, out_bias, w_values, w_gates, w_out_gate, w_out, counts = held
    for copy in copies:
        copy.wait()
    vectors = columns(in_gain[...], in_bias[...], out_gain[...], out_bias[...])
    cols[...] = vectors
    live_all = live_mask(counts)
    tile_x, tile_up = load_tile(pair), load_tile(cotangent)
    for i_hi in range(3):
        lanes = slice(128 * i_hi, 128 * (i_hi + 1))
        x = tile_x[lanes].T
        centre = x - jnp.mean(x, axis=0, keepdims=True)
        inv_std = lax.rsqrt(jnp.mean(centre * centre, axis=0, keepdims=True) + EPS)
        pair_hat = centre * inv_std
        hat[:, lanes] = pair_hat
        inv[:, lanes] = jnp.broadcast_to(inv_std, (8, 128))
        normed_b = (pair_hat * vectors[:, 0:1] + vectors[:, 1:2]).astype(BF16)
        vals = dot(w_values[...], normed_b, (0, 0))
        sig = jax.nn.sigmoid(dot(w_gates[...], normed_b, (0, 0)))
        sig_live = sig * third(live_all, i_hi)
        out = sig_live * vals
        rows[pl.ds(i_hi, 128, stride=6), :] = out[:128]
        rows[pl.ds(3 + i_hi, 128, stride=6), :] = out[128:]
        to_values[:, lanes] = sig_live
        to_gates[:, lanes] = out * (1.0 - sig)
        sig = jax.nn.sigmoid(dot(w_out_gate[...], normed_b, (0, 0)))
        up = tile_up[lanes].T
        out_sig[:, lanes] = sig
        upstream[:, lanes] = up.astype(BF16)
        scaled[:, lanes] = dot(w_out[...], (up * sig).astype(BF16), (1, 0)) * vectors[:, 2:3]
    both[...] = rows[:768].astype(BF16)


def split_kernel(both, left, right, rows, natural):
    rows[:768] = both[...].astype(F32)
    matrix = to_matrix(rows, 3, 6)
    packed = []
    for t in range(3):
        natural[t, :96] = third(matrix, t)
        packed += [jnp.concatenate([natural[t, pl.ds(slot, LOW, stride=12), :] for slot in range(12)], axis=0)]
    packed = jnp.concatenate(packed, axis=1).astype(BF16)
    for part in range(4):
        right[part] = packed
    left[...] = to_matrix(rows, 0, 6).astype(BF16)


def inner_kernel(left, right, inner, right_all, rows):
    parts = [right[part].astype(F32) for part in range(4)]
    ordered = [parts[part][LOW * slot : LOW * (slot + 1)] for slot in range(12) for part in range(4)]
    ordered = jnp.concatenate(ordered, axis=0).astype(BF16)
    right_all[...] = ordered
    to_rows(dot(left[...], ordered, (1, 1)), rows, 0, 4)
    rows[pl.ds(3, 128, stride=4), :] = jnp.zeros((128, 128), F32)
    inner[...] = rows[:512].astype(BF16)


def norm_kernel(inner, scaled, d_inner, inner_hat, rows):
    rows[:512] = inner[...].astype(F32)
    for i_hi in range(3):
        x = rows[pl.ds(i_hi, 128, stride=4), :]
        centre = x - jnp.mean(x, axis=0, keepdims=True)
        inv_std = lax.rsqrt(jnp.mean(centre * centre, axis=0, keepdims=True) + EPS)
        hat = centre * inv_std
        up = scaled[:, 128 * i_hi : 128 * (i_hi + 1)]
        first_mean = jnp.mean(up, axis=0, keepdims=True)
        second_mean = jnp.mean(up * hat, axis=0, keepdims=True)
        rows[pl.ds(i_hi, 128, stride=4), :] = inv_std * (up - first_mean - hat * second_mean)
        inner_hat[:, 128 * i_hi : 128 * (i_hi + 1)] = hat
    d_inner[...] = rows[:512].astype(BF16)


def grad_kernel(d_inner, left, right_all, d_left, d_right, rows):
    rows[:512] = d_inner[...].astype(F32)
    packed = to_matrix(rows, 0, 4).astype(BF16)
    sums = dot(packed, left[...], (0, 0))
    for part in range(4):
        bands = [32 * slot + LOW * part for slot in range(12)]
        d_right[part] = jnp.concatenate([sums[band : band + LOW] for band in bands], axis=0).astype(BF16)
    d_left[...] = dot(packed, right_all[...], (1, 0))


def merge_kernel(d_left, d_right, d_both, rows, natural):
    to_rows(d_left[...], rows, 0, 6)
    parts = [d_right[part].astype(F32) for part in range(4)]
    total = (parts[0] + parts[1]) + (parts[2] + parts[3])
    for t in range(3):
        for slot in range(12):
            natural[t, pl.ds(slot, LOW, stride=12), :] = third(total, t)[LOW * slot : LOW * (slot + 1)]
    to_rows(jnp.concatenate([natural[t, :96] for t in range(3)], axis=1), rows, 3, 6)
    d_both[...] = rows[:768].astype(BF16)


def back_kernel(
    d_both, to_values, to_gates, hat, inv, cols, inner_hat, out_sig, upstream,
    w_values, w_gates, w_out_gate, w_out, update, grad, rows, tile,
):
    vectors = cols[...]
    inner_n = inner_hat[...] * vectors[:, 2:3] + vectors[:, 3:4]
    proj = dot(w_out[...], inner_n.astype(BF16), (0, 0))
    sig = out_sig[...]
    gated = sig * proj
    store_tile(gated.T, tile, update)
    d_gate_out = (upstream[...].astype(F32) * gated * (1.0 - sig)).astype(BF16)
    rows[:768] = d_both[...].astype(F32)
    parts = [
        jnp.concatenate([rows[pl.ds(3 * side + i_hi, 128, stride=6), :] for i_hi in range(3)], axis=1)
        for side in range(2)
    ]
    incoming = jnp.concatenate(parts, axis=0)
    d_values = (incoming * to_values[...]).astype(BF16)
    d_gates = (incoming * to_gates[...]).astype(BF16)
    d_normed = dot(w_out_gate[...], d_gate_out, (1, 0))
    d_normed += dot(w_values[...], d_values, (1, 0)) + dot(w_gates[...], d_gates, (1, 0))
    up = d_normed * vectors[:, 0:1]
    pair_hat = hat[...]
    first_mean = jnp.mean(up, axis=0, keepdims=True)
    second_mean = jnp.mean(up * pair_hat, axis=0, keepdims=True)
    store_tile((inv[:1] * (up - first_mean - pair_hat * second_mean)).T, tile, grad)


def call(kernel, outs, args, scratch=(), last=False):
    vmem = pl.BlockSpec(memory_space=pltpu.VMEM)
    space = jax.ShapeDtypeStruct if last else pltpu.VMEM
    return pl.pallas_call(
        kernel,
        out_shape=[space(*out) for out in outs],
        in_specs=[vmem] * len(args),
        out_specs=[vmem] * len(outs),
        scratch_shapes=[pltpu.VMEM(shape, F32) for shape in scratch],
        compiler_params=pltpu.CompilerParams(vmem_limit_bytes=24 * 1024 * 1024),
    )(*args)


def call_front(outs, args, rows):
    args = [pltpu.with_memory_space_constraint(arg, pltpu.HBM) for arg in args]
    spaces = [pltpu.VMEM] * (len(args) - 1) + [pltpu.SMEM]
    held = [space(arg.shape, arg.dtype) for space, arg in zip(spaces, args)]
    return pl.pallas_call(
        front_kernel,
        out_shape=[pltpu.VMEM(*out) for out in outs],
        in_specs=[pl.BlockSpec(memory_space=pltpu.HBM)] * len(args),
        out_specs=[pl.BlockSpec(memory_space=pltpu.VMEM)] * len(outs),
        scratch_shapes=[pltpu.VMEM(rows, F32)] + held + [pltpu.SemaphoreType.DMA((len(args),))],
        compiler_params=pltpu.CompilerParams(vmem_limit_bytes=24 * 1024 * 1024),
    )(*args)


def exchange(rows):
    return lax.all_to_all(rows.reshape(128, -1, 2, 128), GROUP, 0, 0).reshape(rows.shape)


def shards(
    pair,
    cotangent,
    chain_counts,
    in_gain,
    in_bias,
    w_values,
    w_gates,
    w_out_gate,
    out_gain,
    out_bias,
    w_out,
):
    pair, cotangent = pair.transpose(1, 0, 2), cotangent.transpose(1, 0, 2)
    wide, tall, tile = (256, 384), (128, 384), (12, 24, 128)
    one, two = (512, 128), (768, 128)
    one_rows, two_rows, natural = (520, 128), (776, 128), (3, 112, 128)
    vectors = [vector.reshape(1, 128) for vector in (in_gain, in_bias, out_gain, out_bias)]
    both, scaled, out_sig, upstream, to_values, to_gates, hat, inv, cols = call_front(
        [(two, BF16)]
        + [(tall, F32)] * 2
        + [(tall, BF16)]
        + [(wide, F32)] * 2
        + [(tall, F32), ((8, 384), F32), ((128, 128), F32)],
        [pair, cotangent, *vectors, w_values, w_gates, w_out_gate, w_out, chain_counts],
        two_rows,
    )
    both = exchange(both)
    left, right = call(
        split_kernel, [((96, 384), BF16), ((4, 96, 384), BF16)], [both], [two_rows, natural]
    )
    right = lax.all_to_all(right, "x", 0, 0)
    inner, right = call(inner_kernel, [(one, BF16), ((384, 384), BF16)], [left, right], [one_rows])
    inner = exchange(inner)
    d_inner, inner_hat = call(norm_kernel, [(one, BF16), (tall, F32)], [inner, scaled], [one_rows])
    d_inner = exchange(d_inner)
    d_left, d_right = call(
        grad_kernel, [((96, 384), F32), ((4, 96, 384), BF16)], [d_inner, left, right], [one_rows]
    )
    d_right = lax.all_to_all(d_right, "x", 0, 0)
    (d_both,) = call(merge_kernel, [(two, BF16)], [d_left, d_right], [two_rows, natural])
    d_both = exchange(d_both)
    update, grad = call(
        back_kernel,
        [(tile, BF16)] * 2,
        [
            d_both, to_values, to_gates, hat, inv, cols, inner_hat, out_sig, upstream,
            w_values, w_gates, w_out_gate, w_out,
        ],
        [two_rows, tile],
        last=True,
    )
    return (update.transpose(1, 0, 2), grad.transpose(1, 0, 2))


def solution(mesh):
    fine = Mesh(mesh.devices.reshape(4, 4, 8, 2, 2), ROW + COL)
    placed = P(ROW, COL, None)
    return jax.shard_map(
        shards,
        mesh=fine,
        in_specs=(placed, placed) + (P(),) * 9,
        out_specs=(placed, placed),
        check_vma=False,
    )
```

```python
import jax
import jax.numpy as jnp
from jax import lax
from jax.experimental import pallas as pl
from jax.experimental.pallas import tpu as pltpu
from jax.sharding import Mesh
from jax.sharding import PartitionSpec as P

EPS = 1e-05
F32 = jnp.float32
BF16 = jnp.bfloat16
ROW = ("x", "z_lo")
COL = ("y", "z_hi", "core")
GROUP = ("z_lo",) + COL
SLOTS = 16
LOW = 8


def dot(a, b, contract):
    return lax.dot_general(a, b, ((contract[:1], contract[1:]), ((), ())), preferred_element_type=F32)


def swap_quads(quad):
    return [jnp.concatenate([part[:, 32 * b : 32 * (b + 1)] for part in quad], axis=1) for b in range(4)]


def to_matrix(rows, first, per):
    bands = {}
    for i_hi in range(3):
        turned = rows[pl.ds(first + i_hi, 128, stride=per), :].T
        for j_hi in range(3):
            parts = [turned[LOW * (4 * j_hi + j_lo) : LOW * (4 * j_hi + j_lo + 1)] for j_lo in range(4)]
            for z, part in enumerate(swap_quads(parts)):
                bands[z, i_hi, j_hi] = part
    return jnp.concatenate(
        [
            jnp.concatenate([bands[z, i_hi, j_hi] for j_hi in range(3)], axis=1)
            for z in range(4)
            for i_hi in range(3)
        ],
        axis=0,
    )


def to_rows(matrix, rows, first, per):
    pieces = [(i_hi, j_hi) for i_hi in range(3) for j_hi in range(3)]
    quad = []
    for z in range(4):
        bands = [
            matrix[24 * z + LOW * i_hi : 24 * z + LOW * (i_hi + 1), 128 * j_hi : 128 * (j_hi + 1)]
            for i_hi, j_hi in pieces
        ]
        quad += [jnp.concatenate(bands, axis=0)]
    quad = swap_quads(quad)
    for i_hi in range(3):
        parts = [part[LOW * n : LOW * (n + 1)] for n in range(3 * i_hi, 3 * i_hi + 3) for part in quad]
        parts += [jnp.zeros(((SLOTS - 12) * LOW, 128), F32)]
        rows[pl.ds(first + i_hi, 128, stride=per), :] = jnp.concatenate(parts, axis=0).T


def live_mask(counts):
    valid = counts[0] + counts[1] + counts[2] + counts[3]
    lane = lax.broadcasted_iota(jnp.int32, (1, 384), 1)
    i, j = lane // 128 * LOW + lane % LOW, lane % 128 // LOW
    row = lax.axis_index("x") * 4 + lax.axis_index("z_lo")
    col = lax.axis_index("y") * 4 + lax.axis_index("z_hi") * 2 + lax.axis_index("core")
    live = (row * 24 + i < valid) & (col * 12 + j < valid) & (j < 12)
    return live.astype(F32)


def columns(*vectors):
    spare = jnp.zeros((128 - len(vectors), 128), F32)
    return jnp.concatenate([*vectors, spare], axis=0).T


def load_tile(tile):
    x = tile[...].astype(F32)
    gap = jnp.zeros(((SLOTS - 12) * LOW, 128), F32)
    parts = []
    for i_hi in range(3):
        parts += [x[:, LOW * i_hi : LOW * (i_hi + 1)].reshape(12 * LOW, 128), gap]
    return jnp.concatenate(parts, axis=0)


def store_tile(value, scratch, tile):
    for i_hi in range(3):
        part = value[128 * i_hi : 128 * i_hi + 12 * LOW].reshape(12, LOW, 128)
        scratch[:, LOW * i_hi : LOW * (i_hi + 1), :] = part
    tile[...] = scratch[...].astype(BF16)


def third(value, i_hi):
    return value[:, 128 * i_hi : 128 * (i_hi + 1)]


def front_kernel(*refs):
    ends, (both, normed, to_values, to_gates, hat, inv, cols) = refs[:8], refs[8:15]
    rows, held, sems = refs[15], refs[16:24], refs[24]
    copies = [pltpu.make_async_copy(src, dst, sems.at[n]) for n, (src, dst) in enumerate(zip(ends, held))]
    for copy in copies:
        copy.start()
    pair, in_gain, in_bias, out_gain, out_bias, w_values, w_gates, counts = held
    for copy in copies:
        copy.wait()
    vectors = columns(in_gain[...], in_bias[...], out_gain[...], out_bias[...])
    cols[...] = vectors
    live_all = live_mask(counts)
    tile_x = load_tile(pair)
    for i_hi in range(3):
        lanes = slice(128 * i_hi, 128 * (i_hi + 1))
        x = tile_x[lanes].T
        centre = x - jnp.mean(x, axis=0, keepdims=True)
        inv_std = lax.rsqrt(jnp.mean(centre * centre, axis=0, keepdims=True) + EPS)
        pair_hat = centre * inv_std
        hat[:, lanes] = pair_hat
        inv[:, lanes] = jnp.broadcast_to(inv_std, (8, 128))
        normed_b = (pair_hat * vectors[:, 0:1] + vectors[:, 1:2]).astype(BF16)
        normed[:, lanes] = normed_b
        vals = dot(w_values[...], normed_b, (0, 0))
        sig = jax.nn.sigmoid(dot(w_gates[...], normed_b, (0, 0)))
        sig_live = sig * third(live_all, i_hi)
        out = sig_live * vals
        rows[pl.ds(i_hi, 128, stride=6), :] = out[:128]
        rows[pl.ds(3 + i_hi, 128, stride=6), :] = out[128:]
        to_values[:, lanes] = sig_live
        to_gates[:, lanes] = out * (1.0 - sig)
    both[...] = rows[:768].astype(BF16)


def split_kernel(
    both, normed, cotangent, w_out_gate, w_out, cols, left, right, scaled, out_sig, upstream, rows, natural
):
    sig = jax.nn.sigmoid(dot(w_out_gate[...], normed[...], (0, 0)))
    up = load_tile(cotangent).T
    out_sig[...] = sig
    upstream[...] = up.astype(BF16)
    scaled[...] = dot(w_out[...], (up * sig).astype(BF16), (1, 0)) * cols[:, 2:3]
    rows[:768] = both[...].astype(F32)
    matrix = to_matrix(rows, 3, 6)
    packed = []
    for t in range(3):
        natural[t, :96] = third(matrix, t)
        packed += [jnp.concatenate([natural[t, pl.ds(slot, LOW, stride=12), :] for slot in range(12)], axis=0)]
    packed = jnp.concatenate(packed, axis=1).astype(BF16)
    for part in range(4):
        right[part] = packed
    left[...] = to_matrix(rows, 0, 6).astype(BF16)


def inner_kernel(left, right, inner, right_all, rows):
    parts = [right[part].astype(F32) for part in range(4)]
    ordered = [parts[part][LOW * slot : LOW * (slot + 1)] for slot in range(12) for part in range(4)]
    ordered = jnp.concatenate(ordered, axis=0).astype(BF16)
    right_all[...] = ordered
    to_rows(dot(left[...], ordered, (1, 1)), rows, 0, 4)
    rows[pl.ds(3, 128, stride=4), :] = jnp.zeros((128, 128), F32)
    inner[...] = rows[:512].astype(BF16)


def norm_kernel(inner, scaled, d_inner, inner_hat, rows):
    rows[:512] = inner[...].astype(F32)
    for i_hi in range(3):
        x = rows[pl.ds(i_hi, 128, stride=4), :]
        centre = x - jnp.mean(x, axis=0, keepdims=True)
        inv_std = lax.rsqrt(jnp.mean(centre * centre, axis=0, keepdims=True) + EPS)
        hat = centre * inv_std
        up = scaled[:, 128 * i_hi : 128 * (i_hi + 1)]
        first_mean = jnp.mean(up, axis=0, keepdims=True)
        second_mean = jnp.mean(up * hat, axis=0, keepdims=True)
        rows[pl.ds(i_hi, 128, stride=4), :] = inv_std * (up - first_mean - hat * second_mean)
        inner_hat[:, 128 * i_hi : 128 * (i_hi + 1)] = hat
    d_inner[...] = rows[:512].astype(BF16)


def grad_kernel(d_inner, left, right_all, d_left, d_right, rows):
    rows[:512] = d_inner[...].astype(F32)
    packed = to_matrix(rows, 0, 4).astype(BF16)
    sums = dot(packed, left[...], (0, 0))
    for part in range(4):
        bands = [32 * slot + LOW * part for slot in range(12)]
        d_right[part] = jnp.concatenate([sums[band : band + LOW] for band in bands], axis=0).astype(BF16)
    d_left[...] = dot(packed, right_all[...], (1, 0))


def merge_kernel(d_left, d_right, d_both, rows, natural):
    to_rows(d_left[...], rows, 0, 6)
    parts = [d_right[part].astype(F32) for part in range(4)]
    total = (parts[0] + parts[1]) + (parts[2] + parts[3])
    for t in range(3):
        for slot in range(12):
            natural[t, pl.ds(slot, LOW, stride=12), :] = third(total, t)[LOW * slot : LOW * (slot + 1)]
    to_rows(jnp.concatenate([natural[t, :96] for t in range(3)], axis=1), rows, 3, 6)
    d_both[...] = rows[:768].astype(BF16)


def back_kernel(
    d_both, to_values, to_gates, hat, inv, cols, inner_hat, out_sig, upstream,
    w_values, w_gates, w_out_gate, w_out, update, grad, rows, tile,
):
    vectors = cols[...]
    inner_n = inner_hat[...] * vectors[:, 2:3] + vectors[:, 3:4]
    proj = dot(w_out[...], inner_n.astype(BF16), (0, 0))
    sig = out_sig[...]
    gated = sig * proj
    store_tile(gated.T, tile, update)
    d_gate_out = (upstream[...].astype(F32) * gated * (1.0 - sig)).astype(BF16)
    rows[:768] = d_both[...].astype(F32)
    parts = [
        jnp.concatenate([rows[pl.ds(3 * side + i_hi, 128, stride=6), :] for i_hi in range(3)], axis=1)
        for side in range(2)
    ]
    incoming = jnp.concatenate(parts, axis=0)
    d_values = (incoming * to_values[...]).astype(BF16)
    d_gates = (incoming * to_gates[...]).astype(BF16)
    d_normed = dot(w_out_gate[...], d_gate_out, (1, 0))
    d_normed += dot(w_values[...], d_values, (1, 0)) + dot(w_gates[...], d_gates, (1, 0))
    up = d_normed * vectors[:, 0:1]
    pair_hat = hat[...]
    first_mean = jnp.mean(up, axis=0, keepdims=True)
    second_mean = jnp.mean(up * pair_hat, axis=0, keepdims=True)
    store_tile((inv[:1] * (up - first_mean - pair_hat * second_mean)).T, tile, grad)


def call(kernel, outs, args, scratch=(), last=False):
    vmem = pl.BlockSpec(memory_space=pltpu.VMEM)
    space = jax.ShapeDtypeStruct if last else pltpu.VMEM
    return pl.pallas_call(
        kernel,
        out_shape=[space(*out) for out in outs],
        in_specs=[vmem] * len(args),
        out_specs=[vmem] * len(outs),
        scratch_shapes=[pltpu.VMEM(shape, F32) for shape in scratch],
        compiler_params=pltpu.CompilerParams(vmem_limit_bytes=24 * 1024 * 1024),
    )(*args)


def call_front(outs, args, rows):
    args = [pltpu.with_memory_space_constraint(arg, pltpu.HBM) for arg in args]
    spaces = [pltpu.VMEM] * (len(args) - 1) + [pltpu.SMEM]
    held = [space(arg.shape, arg.dtype) for space, arg in zip(spaces, args)]
    return pl.pallas_call(
        front_kernel,
        out_shape=[pltpu.VMEM(*out) for out in outs],
        in_specs=[pl.BlockSpec(memory_space=pltpu.HBM)] * len(args),
        out_specs=[pl.BlockSpec(memory_space=pltpu.VMEM)] * len(outs),
        scratch_shapes=[pltpu.VMEM(rows, F32)] + held + [pltpu.SemaphoreType.DMA((len(args),))],
        compiler_params=pltpu.CompilerParams(vmem_limit_bytes=24 * 1024 * 1024),
    )(*args)


def exchange(rows):
    return lax.all_to_all(rows.reshape(128, -1, 2, 128), GROUP, 0, 0).reshape(rows.shape)


def shards(
    pair,
    cotangent,
    chain_counts,
    in_gain,
    in_bias,
    w_values,
    w_gates,
    w_out_gate,
    out_gain,
    out_bias,
    w_out,
):
    pair, cotangent = pair.transpose(1, 0, 2), cotangent.transpose(1, 0, 2)
    wide, tall, tile = (256, 384), (128, 384), (12, 24, 128)
    one, two = (512, 128), (768, 128)
    one_rows, two_rows, natural = (520, 128), (776, 128), (3, 112, 128)
    vectors = [vector.reshape(1, 128) for vector in (in_gain, in_bias, out_gain, out_bias)]
    both, normed, to_values, to_gates, hat, inv, cols = call_front(
        [(two, BF16), (tall, BF16)]
        + [(wide, F32)] * 2
        + [(tall, F32), ((8, 384), F32), ((128, 128), F32)],
        [pair, *vectors, w_values, w_gates, chain_counts],
        two_rows,
    )
    both = exchange(both)
    left, right, scaled, out_sig, upstream = call(
        split_kernel,
        [((96, 384), BF16), ((4, 96, 384), BF16), (tall, F32), (tall, F32), (tall, BF16)],
        [both, normed, cotangent, w_out_gate, w_out, cols],
        [two_rows, natural],
    )
    right = lax.all_to_all(right, "x", 0, 0)
    inner, right = call(inner_kernel, [(one, BF16), ((384, 384), BF16)], [left, right], [one_rows])
    inner = exchange(inner)
    d_inner, inner_hat = call(norm_kernel, [(one, BF16), (tall, F32)], [inner, scaled], [one_rows])
    d_inner = exchange(d_inner)
    d_left, d_right = call(
        grad_kernel, [((96, 384), F32), ((4, 96, 384), BF16)], [d_inner, left, right], [one_rows]
    )
    d_right = lax.all_to_all(d_right, "x", 0, 0)
    (d_both,) = call(merge_kernel, [(two, BF16)], [d_left, d_right], [two_rows, natural])
    d_both = exchange(d_both)
    update, grad = call(
        back_kernel,
        [(tile, BF16)] * 2,
        [
            d_both, to_values, to_gates, hat, inv, cols, inner_hat, out_sig, upstream,
            w_values, w_gates, w_out_gate, w_out,
        ],
        [two_rows, tile],
        last=True,
    )
    return (update.transpose(1, 0, 2), grad.transpose(1, 0, 2))


def solution(mesh):
    fine = Mesh(mesh.devices.reshape(4, 4, 8, 2, 2), ROW + COL)
    placed = P(ROW, COL, None)
    return jax.shard_map(
        shards,
        mesh=fine,
        in_specs=(placed, placed) + (P(),) * 9,
        out_specs=(placed, placed),
        check_vma=False,
    )
```

```python
import jax
import jax.numpy as jnp
from jax import lax
from jax.experimental import pallas as pl
from jax.experimental.pallas import tpu as pltpu
from jax.sharding import Mesh
from jax.sharding import PartitionSpec as P

EPS = 1e-05
F32 = jnp.float32
BF16 = jnp.bfloat16
ROW = ("x", "z_lo")
COL = ("y", "z_hi", "core")
GROUP = ("z_lo",) + COL
SLOTS = 16
LOW = 8


def dot(a, b, contract):
    return lax.dot_general(a, b, ((contract[:1], contract[1:]), ((), ())), preferred_element_type=F32)


def swap_quads(quad):
    return [jnp.concatenate([part[:, 32 * b : 32 * (b + 1)] for part in quad], axis=1) for b in range(4)]


def to_matrix(rows, first, per):
    bands = {}
    for i_hi in range(3):
        turned = rows[pl.ds(first + i_hi, 128, stride=per), :].T
        for j_hi in range(3):
            parts = [turned[LOW * (4 * j_hi + j_lo) : LOW * (4 * j_hi + j_lo + 1)] for j_lo in range(4)]
            for z, part in enumerate(swap_quads(parts)):
                bands[z, i_hi, j_hi] = part
    return jnp.concatenate(
        [
            jnp.concatenate([bands[z, i_hi, j_hi] for j_hi in range(3)], axis=1)
            for z in range(4)
            for i_hi in range(3)
        ],
        axis=0,
    )


def to_rows(matrix, rows, first, per):
    pieces = [(i_hi, j_hi) for i_hi in range(3) for j_hi in range(3)]
    quad = []
    for z in range(4):
        bands = [
            matrix[24 * z + LOW * i_hi : 24 * z + LOW * (i_hi + 1), 128 * j_hi : 128 * (j_hi + 1)]
            for i_hi, j_hi in pieces
        ]
        quad += [jnp.concatenate(bands, axis=0)]
    quad = swap_quads(quad)
    for i_hi in range(3):
        parts = [part[LOW * n : LOW * (n + 1)] for n in range(3 * i_hi, 3 * i_hi + 3) for part in quad]
        parts += [jnp.zeros(((SLOTS - 12) * LOW, 128), F32)]
        rows[pl.ds(first + i_hi, 128, stride=per), :] = jnp.concatenate(parts, axis=0).T


def live_mask(counts):
    valid = counts[0] + counts[1] + counts[2] + counts[3]
    lane = lax.broadcasted_iota(jnp.int32, (1, 384), 1)
    i, j = lane // 128 * LOW + lane % LOW, lane % 128 // LOW
    row = lax.axis_index("x") * 4 + lax.axis_index("z_lo")
    col = lax.axis_index("y") * 4 + lax.axis_index("z_hi") * 2 + lax.axis_index("core")
    live = (row * 24 + i < valid) & (col * 12 + j < valid) & (j < 12)
    return live.astype(F32)


def columns(*vectors):
    spare = jnp.zeros((128 - len(vectors), 128), F32)
    return jnp.concatenate([*vectors, spare], axis=0).T


def load_tile(tile):
    x = tile[...].astype(F32)
    gap = jnp.zeros(((SLOTS - 12) * LOW, 128), F32)
    parts = []
    for i_hi in range(3):
        parts += [x[:, LOW * i_hi : LOW * (i_hi + 1)].reshape(12 * LOW, 128), gap]
    return jnp.concatenate(parts, axis=0)


def store_tile(value, scratch, tile):
    for i_hi in range(3):
        part = value[128 * i_hi : 128 * i_hi + 12 * LOW].reshape(12, LOW, 128)
        scratch[:, LOW * i_hi : LOW * (i_hi + 1), :] = part
    tile[...] = scratch[...].astype(BF16)


def third(value, i_hi):
    return value[:, 128 * i_hi : 128 * (i_hi + 1)]


def front_kernel(*refs):
    ends, (both, normed, to_values, to_gates, hat, inv, cols) = refs[:8], refs[8:15]
    rows, held, sems = refs[15], refs[16:24], refs[24]
    copies = [pltpu.make_async_copy(src, dst, sems.at[n]) for n, (src, dst) in enumerate(zip(ends, held))]
    for copy in copies:
        copy.start()
    pair, in_gain, in_bias, out_gain, out_bias, w_values, w_gates, counts = held
    for copy in copies:
        copy.wait()
    vectors = columns(in_gain[...], in_bias[...], out_gain[...], out_bias[...])
    cols[...] = vectors
    live_all = live_mask(counts)
    tile_x = load_tile(pair)
    for i_hi in range(3):
        lanes = slice(128 * i_hi, 128 * (i_hi + 1))
        x = tile_x[lanes].T
        centre = x - jnp.mean(x, axis=0, keepdims=True)
        inv_std = lax.rsqrt(jnp.mean(centre * centre, axis=0, keepdims=True) + EPS)
        pair_hat = centre * inv_std
        hat[:, lanes] = pair_hat
        inv[:, lanes] = jnp.broadcast_to(inv_std, (8, 128))
        normed_b = (pair_hat * vectors[:, 0:1] + vectors[:, 1:2]).astype(BF16)
        normed[:, lanes] = normed_b
        vals = dot(w_values[...], normed_b, (0, 0))
        sig = jax.nn.sigmoid(dot(w_gates[...], normed_b, (0, 0)))
        sig_live = sig * third(live_all, i_hi)
        out = sig_live * vals
        rows[pl.ds(i_hi, 128, stride=6), :] = out[:128]
        rows[pl.ds(3 + i_hi, 128, stride=6), :] = out[128:]
        to_values[:, lanes] = sig_live
        to_gates[:, lanes] = out * (1.0 - sig)
    both[...] = rows[:768].astype(BF16)


def split_kernel(
    both, normed, cotangent, w_out_gate, w_out, cols, left, right, scaled, out_sig, upstream, rows, natural
):
    sig = jax.nn.sigmoid(dot(w_out_gate[...], normed[...], (0, 0)))
    up = load_tile(cotangent).T
    out_sig[...] = sig
    upstream[...] = up.astype(BF16)
    scaled[...] = dot(w_out[...], (up * sig).astype(BF16), (1, 0)) * cols[:, 2:3]
    rows[:768] = both[...].astype(F32)
    matrix = to_matrix(rows, 3, 6)
    packed = []
    for t in range(3):
        natural[t, :96] = third(matrix, t)
        packed += [jnp.concatenate([natural[t, pl.ds(slot, LOW, stride=12), :] for slot in range(12)], axis=0)]
    packed = jnp.concatenate(packed, axis=1).astype(BF16)
    for part in range(4):
        right[part] = packed
    left[...] = to_matrix(rows, 0, 6).astype(BF16)


def inner_kernel(left, right, inner, right_all, rows):
    parts = [right[part].astype(F32) for part in range(4)]
    ordered = [parts[part][LOW * slot : LOW * (slot + 1)] for slot in range(12) for part in range(4)]
    ordered = jnp.concatenate(ordered, axis=0).astype(BF16)
    right_all[...] = ordered
    to_rows(dot(left[...], ordered, (1, 1)), rows, 0, 4)
    rows[pl.ds(3, 128, stride=4), :] = jnp.zeros((128, 128), F32)
    inner[...] = rows[:512].astype(BF16)


def norm_kernel(inner, scaled, d_inner, inner_hat, rows):
    rows[:512] = inner[...].astype(F32)
    for i_hi in range(3):
        x = rows[pl.ds(i_hi, 128, stride=4), :]
        centre = x - jnp.mean(x, axis=0, keepdims=True)
        inv_std = lax.rsqrt(jnp.mean(centre * centre, axis=0, keepdims=True) + EPS)
        hat = centre * inv_std
        up = scaled[:, 128 * i_hi : 128 * (i_hi + 1)]
        first_mean = jnp.mean(up, axis=0, keepdims=True)
        second_mean = jnp.mean(up * hat, axis=0, keepdims=True)
        rows[pl.ds(i_hi, 128, stride=4), :] = inv_std * (up - first_mean - hat * second_mean)
        inner_hat[:, 128 * i_hi : 128 * (i_hi + 1)] = hat
    d_inner[...] = rows[:512].astype(BF16)


def grad_kernel(d_inner, left, right_all, d_left, d_right, rows):
    rows[:512] = d_inner[...].astype(F32)
    packed = to_matrix(rows, 0, 4).astype(BF16)
    sums = dot(packed, left[...], (0, 0))
    for part in range(4):
        bands = [32 * slot + LOW * part for slot in range(12)]
        d_right[part] = jnp.concatenate([sums[band : band + LOW] for band in bands], axis=0).astype(BF16)
    d_left[...] = dot(packed, right_all[...], (1, 0))


def merge_kernel(
    d_left, d_right, inner_hat, out_sig, upstream, cols, w_out, w_out_gate, d_both, gated, d_out, rows, natural
):
    inner_n = inner_hat[...] * cols[:, 2:3] + cols[:, 3:4]
    proj = dot(w_out[...], inner_n.astype(BF16), (0, 0))
    sig = out_sig[...]
    product = sig * proj
    gated[...] = product
    d_gate_out = (upstream[...].astype(F32) * product * (1.0 - sig)).astype(BF16)
    d_out[...] = dot(w_out_gate[...], d_gate_out, (1, 0))
    to_rows(d_left[...], rows, 0, 6)
    parts = [d_right[part].astype(F32) for part in range(4)]
    total = (parts[0] + parts[1]) + (parts[2] + parts[3])
    for t in range(3):
        for slot in range(12):
            natural[t, pl.ds(slot, LOW, stride=12), :] = third(total, t)[LOW * slot : LOW * (slot + 1)]
    to_rows(jnp.concatenate([natural[t, :96] for t in range(3)], axis=1), rows, 3, 6)
    d_both[...] = rows[:768].astype(BF16)


def back_kernel(
    d_both, to_values, to_gates, hat, inv, cols, gated, d_out, w_values, w_gates, update, grad, rows, tile
):
    store_tile(gated[...].T, tile, update)
    rows[:768] = d_both[...].astype(F32)
    parts = [
        jnp.concatenate([rows[pl.ds(3 * side + i_hi, 128, stride=6), :] for i_hi in range(3)], axis=1)
        for side in range(2)
    ]
    incoming = jnp.concatenate(parts, axis=0)
    d_values = (incoming * to_values[...]).astype(BF16)
    d_gates = (incoming * to_gates[...]).astype(BF16)
    d_normed = d_out[...] + dot(w_values[...], d_values, (1, 0)) + dot(w_gates[...], d_gates, (1, 0))
    up = d_normed * cols[:, 0:1]
    pair_hat = hat[...]
    first_mean = jnp.mean(up, axis=0, keepdims=True)
    second_mean = jnp.mean(up * pair_hat, axis=0, keepdims=True)
    store_tile((inv[:1] * (up - first_mean - pair_hat * second_mean)).T, tile, grad)


def call(kernel, outs, args, scratch=(), last=False):
    vmem = pl.BlockSpec(memory_space=pltpu.VMEM)
    space = jax.ShapeDtypeStruct if last else pltpu.VMEM
    return pl.pallas_call(
        kernel,
        out_shape=[space(*out) for out in outs],
        in_specs=[vmem] * len(args),
        out_specs=[vmem] * len(outs),
        scratch_shapes=[pltpu.VMEM(shape, F32) for shape in scratch],
        compiler_params=pltpu.CompilerParams(vmem_limit_bytes=24 * 1024 * 1024),
    )(*args)


def call_front(outs, args, rows):
    args = [pltpu.with_memory_space_constraint(arg, pltpu.HBM) for arg in args]
    spaces = [pltpu.VMEM] * (len(args) - 1) + [pltpu.SMEM]
    held = [space(arg.shape, arg.dtype) for space, arg in zip(spaces, args)]
    return pl.pallas_call(
        front_kernel,
        out_shape=[pltpu.VMEM(*out) for out in outs],
        in_specs=[pl.BlockSpec(memory_space=pltpu.HBM)] * len(args),
        out_specs=[pl.BlockSpec(memory_space=pltpu.VMEM)] * len(outs),
        scratch_shapes=[pltpu.VMEM(rows, F32)] + held + [pltpu.SemaphoreType.DMA((len(args),))],
        compiler_params=pltpu.CompilerParams(vmem_limit_bytes=24 * 1024 * 1024),
    )(*args)


def exchange(rows):
    return lax.all_to_all(rows.reshape(128, -1, 2, 128), GROUP, 0, 0).reshape(rows.shape)


def shards(
    pair,
    cotangent,
    chain_counts,
    in_gain,
    in_bias,
    w_values,
    w_gates,
    w_out_gate,
    out_gain,
    out_bias,
    w_out,
):
    pair, cotangent = pair.transpose(1, 0, 2), cotangent.transpose(1, 0, 2)
    wide, tall, tile = (256, 384), (128, 384), (12, 24, 128)
    one, two = (512, 128), (768, 128)
    one_rows, two_rows, natural = (520, 128), (776, 128), (3, 112, 128)
    vectors = [vector.reshape(1, 128) for vector in (in_gain, in_bias, out_gain, out_bias)]
    both, normed, to_values, to_gates, hat, inv, cols = call_front(
        [(two, BF16), (tall, BF16)]
        + [(wide, F32)] * 2
        + [(tall, F32), ((8, 384), F32), ((128, 128), F32)],
        [pair, *vectors, w_values, w_gates, chain_counts],
        two_rows,
    )
    both = exchange(both)
    left, right, scaled, out_sig, upstream = call(
        split_kernel,
        [((96, 384), BF16), ((4, 96, 384), BF16), (tall, F32), (tall, F32), (tall, BF16)],
        [both, normed, cotangent, w_out_gate, w_out, cols],
        [two_rows, natural],
    )
    right = lax.all_to_all(right, "x", 0, 0)
    inner, right = call(inner_kernel, [(one, BF16), ((384, 384), BF16)], [left, right], [one_rows])
    inner = exchange(inner)
    d_inner, inner_hat = call(norm_kernel, [(one, BF16), (tall, F32)], [inner, scaled], [one_rows])
    d_inner = exchange(d_inner)
    d_left, d_right = call(
        grad_kernel, [((96, 384), F32), ((4, 96, 384), BF16)], [d_inner, left, right], [one_rows]
    )
    d_right = lax.all_to_all(d_right, "x", 0, 0)
    d_both, gated, d_out = call(
        merge_kernel,
        [(two, BF16), (tall, F32), (tall, F32)],
        [d_left, d_right, inner_hat, out_sig, upstream, cols, w_out, w_out_gate],
        [two_rows, natural],
    )
    d_both = exchange(d_both)
    update, grad = call(
        back_kernel,
        [(tile, BF16)] * 2,
        [d_both, to_values, to_gates, hat, inv, cols, gated, d_out, w_values, w_gates],
        [two_rows, tile],
        last=True,
    )
    return (update.transpose(1, 0, 2), grad.transpose(1, 0, 2))


def solution(mesh):
    fine = Mesh(mesh.devices.reshape(4, 4, 8, 2, 2), ROW + COL)
    placed = P(ROW, COL, None)
    return jax.shard_map(
        shards,
        mesh=fine,
        in_specs=(placed, placed) + (P(),) * 9,
        out_specs=(placed, placed),
        check_vma=False,
    )
```

```python
import jax
import jax.numpy as jnp
from jax import lax
from jax.experimental import pallas as pl
from jax.experimental.pallas import tpu as pltpu
from jax.sharding import Mesh
from jax.sharding import PartitionSpec as P

EPS = 1e-05
F32 = jnp.float32
BF16 = jnp.bfloat16
ROW = ("x", "z_lo")
COL = ("y", "z_hi", "core")
GROUP = ("z_lo",) + COL
SLOTS = 16
LOW = 8


def dot(a, b, contract):
    return lax.dot_general(a, b, ((contract[:1], contract[1:]), ((), ())), preferred_element_type=F32)


def swap_quads(quad):
    return [jnp.concatenate([part[:, 32 * b : 32 * (b + 1)] for part in quad], axis=1) for b in range(4)]


def to_matrix(rows, first, per):
    bands = {}
    for i_hi in range(3):
        turned = rows[pl.ds(first + i_hi, 128, stride=per), :].T
        for j_hi in range(3):
            parts = [turned[LOW * (4 * j_hi + j_lo) : LOW * (4 * j_hi + j_lo + 1)] for j_lo in range(4)]
            for z, part in enumerate(swap_quads(parts)):
                bands[z, i_hi, j_hi] = part
    return jnp.concatenate(
        [
            jnp.concatenate([bands[z, i_hi, j_hi] for j_hi in range(3)], axis=1)
            for z in range(4)
            for i_hi in range(3)
        ],
        axis=0,
    )


def to_rows(matrix, rows, first, per):
    pieces = [(i_hi, j_hi) for i_hi in range(3) for j_hi in range(3)]
    quad = []
    for z in range(4):
        bands = [
            matrix[24 * z + LOW * i_hi : 24 * z + LOW * (i_hi + 1), 128 * j_hi : 128 * (j_hi + 1)]
            for i_hi, j_hi in pieces
        ]
        quad += [jnp.concatenate(bands, axis=0)]
    quad = swap_quads(quad)
    for i_hi in range(3):
        parts = [part[LOW * n : LOW * (n + 1)] for n in range(3 * i_hi, 3 * i_hi + 3) for part in quad]
        parts += [jnp.zeros(((SLOTS - 12) * LOW, 128), F32)]
        rows[pl.ds(first + i_hi, 128, stride=per), :] = jnp.concatenate(parts, axis=0).T


def live_mask(counts):
    valid = counts[0] + counts[1] + counts[2] + counts[3]
    lane = lax.broadcasted_iota(jnp.int32, (1, 384), 1)
    i, j = lane // 128 * LOW + lane % LOW, lane % 128 // LOW
    row = lax.axis_index("x") * 4 + lax.axis_index("z_lo")
    col = lax.axis_index("y") * 4 + lax.axis_index("z_hi") * 2 + lax.axis_index("core")
    live = (row * 24 + i < valid) & (col * 12 + j < valid) & (j < 12)
    return live.astype(F32)


def columns(*vectors):
    spare = jnp.zeros((128 - len(vectors), 128), F32)
    return jnp.concatenate([*vectors, spare], axis=0).T


def load_tile(tile):
    x = tile[...].astype(F32)
    gap = jnp.zeros(((SLOTS - 12) * LOW, 128), F32)
    parts = []
    for i_hi in range(3):
        parts += [x[:, LOW * i_hi : LOW * (i_hi + 1)].reshape(12 * LOW, 128), gap]
    return jnp.concatenate(parts, axis=0)


def store_tile(value, scratch, tile):
    for i_hi in range(3):
        part = value[128 * i_hi : 128 * i_hi + 12 * LOW].reshape(12, LOW, 128)
        scratch[:, LOW * i_hi : LOW * (i_hi + 1), :] = part
    tile[...] = scratch[...].astype(BF16)


def third(value, i_hi):
    return value[:, 128 * i_hi : 128 * (i_hi + 1)]


def front_kernel(*refs):
    ends, (both, normed, to_values, to_gates, hat, inv, cols) = refs[:8], refs[8:15]
    rows, held, sems = refs[15], refs[16:24], refs[24]
    copies = [pltpu.make_async_copy(src, dst, sems.at[n]) for n, (src, dst) in enumerate(zip(ends, held))]
    for copy in copies:
        copy.start()
    pair, in_gain, in_bias, out_gain, out_bias, w_values, w_gates, counts = held
    for copy in copies:
        copy.wait()
    vectors = columns(in_gain[...], in_bias[...], out_gain[...], out_bias[...])
    cols[...] = vectors
    live_all = live_mask(counts)
    tile_x = load_tile(pair)
    for i_hi in range(3):
        lanes = slice(128 * i_hi, 128 * (i_hi + 1))
        x = tile_x[lanes].T
        centre = x - jnp.mean(x, axis=0, keepdims=True)
        inv_std = lax.rsqrt(jnp.mean(centre * centre, axis=0, keepdims=True) + EPS)
        pair_hat = centre * inv_std
        hat[:, lanes] = pair_hat
        inv[:, lanes] = jnp.broadcast_to(inv_std, (8, 128))
        normed_b = (pair_hat * vectors[:, 0:1] + vectors[:, 1:2]).astype(BF16)
        normed[:, lanes] = normed_b
        vals = dot(w_values[...], normed_b, (0, 0))
        sig = jax.nn.sigmoid(dot(w_gates[...], normed_b, (0, 0)))
        sig_live = sig * third(live_all, i_hi)
        out = sig_live * vals
        rows[pl.ds(i_hi, 128, stride=6), :] = out[:128]
        rows[pl.ds(3 + i_hi, 128, stride=6), :] = out[128:]
        to_values[:, lanes] = sig_live
        to_gates[:, lanes] = out * (1.0 - sig)
    both[...] = rows[:768].astype(BF16)


def split_kernel(
    both, normed, cotangent, w_out_gate, w_out, cols, left, right, scaled, out_sig, upstream, rows, natural
):
    sig = jax.nn.sigmoid(dot(w_out_gate[...], normed[...], (0, 0)))
    up = load_tile(cotangent).T
    out_sig[...] = sig
    upstream[...] = up.astype(BF16)
    scaled[...] = dot(w_out[...], (up * sig).astype(BF16), (1, 0)) * cols[:, 2:3]
    rows[:768] = both[...].astype(F32)
    matrix = to_matrix(rows, 3, 6)
    packed = []
    for t in range(3):
        natural[t, :96] = third(matrix, t)
        packed += [jnp.concatenate([natural[t, pl.ds(slot, LOW, stride=12), :] for slot in range(12)], axis=0)]
    packed = jnp.concatenate(packed, axis=1).astype(BF16)
    for part in range(4):
        right[part] = packed
    left[...] = to_matrix(rows, 0, 6).astype(BF16)


def inner_kernel(left, right, inner, right_all, rows):
    parts = [right[part].astype(F32) for part in range(4)]
    ordered = [parts[part][LOW * slot : LOW * (slot + 1)] for slot in range(12) for part in range(4)]
    ordered = jnp.concatenate(ordered, axis=0).astype(BF16)
    right_all[...] = ordered
    rows[:512] = jnp.zeros((512, 128), F32)
    to_rows(dot(left[...], ordered, (1, 1)), rows, 0, 4)
    inner[...] = rows[:512].astype(BF16)


def norm_kernel(inner, scaled, d_inner, inner_hat, rows):
    rows[:512] = inner[...].astype(F32)
    for i_hi in range(3):
        x = rows[pl.ds(i_hi, 128, stride=4), :]
        centre = x - jnp.mean(x, axis=0, keepdims=True)
        inv_std = lax.rsqrt(jnp.mean(centre * centre, axis=0, keepdims=True) + EPS)
        hat = centre * inv_std
        up = scaled[:, 128 * i_hi : 128 * (i_hi + 1)]
        first_mean = jnp.mean(up, axis=0, keepdims=True)
        second_mean = jnp.mean(up * hat, axis=0, keepdims=True)
        rows[pl.ds(i_hi, 128, stride=4), :] = inv_std * (up - first_mean - hat * second_mean)
        inner_hat[:, 128 * i_hi : 128 * (i_hi + 1)] = hat
    d_inner[...] = rows[:512].astype(BF16)


def grad_kernel(d_inner, left, right_all, d_left, d_right, rows):
    rows[:512] = d_inner[...].astype(F32)
    packed = to_matrix(rows, 0, 4).astype(BF16)
    sums = dot(packed, left[...], (0, 0))
    for part in range(4):
        bands = [32 * slot + LOW * part for slot in range(12)]
        d_right[part] = jnp.concatenate([sums[band : band + LOW] for band in bands], axis=0).astype(BF16)
    d_left[...] = dot(packed, right_all[...], (1, 0))


def merge_kernel(
    d_left, d_right, inner_hat, out_sig, upstream, cols, w_out, w_out_gate, d_both, gated, d_out, rows, natural
):
    inner_n = inner_hat[...] * cols[:, 2:3] + cols[:, 3:4]
    proj = dot(w_out[...], inner_n.astype(BF16), (0, 0))
    sig = out_sig[...]
    product = sig * proj
    gated[...] = product
    d_gate_out = (upstream[...].astype(F32) * product * (1.0 - sig)).astype(BF16)
    d_out[...] = dot(w_out_gate[...], d_gate_out, (1, 0))
    to_rows(d_left[...], rows, 0, 6)
    parts = [d_right[part].astype(F32) for part in range(4)]
    total = (parts[0] + parts[1]) + (parts[2] + parts[3])
    for t in range(3):
        for slot in range(12):
            natural[t, pl.ds(slot, LOW, stride=12), :] = third(total, t)[LOW * slot : LOW * (slot + 1)]
    to_rows(jnp.concatenate([natural[t, :96] for t in range(3)], axis=1), rows, 3, 6)
    d_both[...] = rows[:768].astype(BF16)


def back_kernel(
    d_both, to_values, to_gates, hat, inv, cols, gated, d_out, w_values, w_gates, update, grad, rows, tile
):
    store_tile(gated[...].T, tile, update)
    rows[:768] = d_both[...].astype(F32)
    parts = [
        jnp.concatenate([rows[pl.ds(3 * side + i_hi, 128, stride=6), :] for i_hi in range(3)], axis=1)
        for side in range(2)
    ]
    incoming = jnp.concatenate(parts, axis=0)
    d_values = (incoming * to_values[...]).astype(BF16)
    d_gates = (incoming * to_gates[...]).astype(BF16)
    d_normed = d_out[...] + dot(w_values[...], d_values, (1, 0)) + dot(w_gates[...], d_gates, (1, 0))
    up = d_normed * cols[:, 0:1]
    pair_hat = hat[...]
    first_mean = jnp.mean(up, axis=0, keepdims=True)
    second_mean = jnp.mean(up * pair_hat, axis=0, keepdims=True)
    store_tile((inv[:1] * (up - first_mean - pair_hat * second_mean)).T, tile, grad)


def call(kernel, outs, args, scratch=(), last=False):
    vmem = pl.BlockSpec(memory_space=pltpu.VMEM)
    space = jax.ShapeDtypeStruct if last else pltpu.VMEM
    return pl.pallas_call(
        kernel,
        out_shape=[space(*out) for out in outs],
        in_specs=[vmem] * len(args),
        out_specs=[vmem] * len(outs),
        scratch_shapes=[pltpu.VMEM(shape, F32) for shape in scratch],
        compiler_params=pltpu.CompilerParams(vmem_limit_bytes=24 * 1024 * 1024),
    )(*args)


def call_front(outs, args, rows):
    args = [pltpu.with_memory_space_constraint(arg, pltpu.HBM) for arg in args]
    spaces = [pltpu.VMEM] * (len(args) - 1) + [pltpu.SMEM]
    held = [space(arg.shape, arg.dtype) for space, arg in zip(spaces, args)]
    return pl.pallas_call(
        front_kernel,
        out_shape=[pltpu.VMEM(*out) for out in outs],
        in_specs=[pl.BlockSpec(memory_space=pltpu.HBM)] * len(args),
        out_specs=[pl.BlockSpec(memory_space=pltpu.VMEM)] * len(outs),
        scratch_shapes=[pltpu.VMEM(rows, F32)] + held + [pltpu.SemaphoreType.DMA((len(args),))],
        compiler_params=pltpu.CompilerParams(vmem_limit_bytes=24 * 1024 * 1024),
    )(*args)


def exchange(rows):
    return lax.all_to_all(rows.reshape(128, -1, 2, 128), GROUP, 0, 0).reshape(rows.shape)


def shards(
    pair,
    cotangent,
    chain_counts,
    in_gain,
    in_bias,
    w_values,
    w_gates,
    w_out_gate,
    out_gain,
    out_bias,
    w_out,
):
    pair, cotangent = pair.transpose(1, 0, 2), cotangent.transpose(1, 0, 2)
    wide, tall, tile = (256, 384), (128, 384), (12, 24, 128)
    one, two = (512, 128), (768, 128)
    one_rows, two_rows, natural = (520, 128), (776, 128), (3, 112, 128)
    vectors = [vector.reshape(1, 128) for vector in (in_gain, in_bias, out_gain, out_bias)]
    both, normed, to_values, to_gates, hat, inv, cols = call_front(
        [(two, BF16), (tall, BF16)]
        + [(wide, F32)] * 2
        + [(tall, F32), ((8, 384), F32), ((128, 128), F32)],
        [pair, *vectors, w_values, w_gates, chain_counts],
        two_rows,
    )
    both = exchange(both)
    left, right, scaled, out_sig, upstream = call(
        split_kernel,
        [((96, 384), BF16), ((4, 96, 384), BF16), (tall, F32), (tall, F32), (tall, BF16)],
        [both, normed, cotangent, w_out_gate, w_out, cols],
        [two_rows, natural],
    )
    right = lax.all_to_all(right, "x", 0, 0)
    inner, right = call(inner_kernel, [(one, BF16), ((384, 384), BF16)], [left, right], [one_rows])
    inner = exchange(inner)
    d_inner, inner_hat = call(norm_kernel, [(one, BF16), (tall, F32)], [inner, scaled], [one_rows])
    d_inner = exchange(d_inner)
    d_left, d_right = call(
        grad_kernel, [((96, 384), F32), ((4, 96, 384), BF16)], [d_inner, left, right], [one_rows]
    )
    d_right = lax.all_to_all(d_right, "x", 0, 0)
    d_both, gated, d_out = call(
        merge_kernel,
        [(two, BF16), (tall, F32), (tall, F32)],
        [d_left, d_right, inner_hat, out_sig, upstream, cols, w_out, w_out_gate],
        [two_rows, natural],
    )
    d_both = exchange(d_both)
    update, grad = call(
        back_kernel,
        [(tile, BF16)] * 2,
        [d_both, to_values, to_gates, hat, inv, cols, gated, d_out, w_values, w_gates],
        [two_rows, tile],
        last=True,
    )
    return (update.transpose(1, 0, 2), grad.transpose(1, 0, 2))


def solution(mesh):
    fine = Mesh(mesh.devices.reshape(4, 4, 8, 2, 2), ROW + COL)
    placed = P(ROW, COL, None)
    return jax.shard_map(
        shards,
        mesh=fine,
        in_specs=(placed, placed) + (P(),) * 9,
        out_specs=(placed, placed),
        check_vma=False,
    )
```
